256 devices in a mesh: dp: 16 (over x_lo, y, core), axial: 16 (over z, x_hi).
Axes of the slice: x: 4 (x_hi: 2, x_lo: 2; x = x_hi * 2 + x_lo), y: 4, z: 8, core: 2. Of those that a mesh axis runs over, the one named last changes fastest.
Arguments:
- homolog_activity: bfloat16 [512, 128, 256], P(('dp', 'axial')), parts along dimension 0, may hold values from -6 to 6
- homolog_symbol_ids: int32 [512, 128], P(('dp', 'axial')), parts along dimension 0, may hold values from 0 to 22
- residue_present_mask: int32 [2048], P('dp'), parts along dimension 0, may hold values 0 or 1
- pair_state: bfloat16 [2048, 128, 128], P(('dp', 'axial')), parts along dimension 0, may hold values from -6 to 6
- pair_valid_mask: int32 [2048, 128], P(('dp', 'axial')), parts along dimension 0, may hold values 0 or 1
- symbol_lookup_matrix: bfloat16 [23, 256], replicated, may hold values from -3 to 3
- row_query_weight: bfloat16 [256, 256], replicated, as said below
- horizontal_attention_matrix: bfloat16 [256, 768], replicated, may hold values from -0.375 to 0.375
- pair_bias_weight: bfloat16 [128, 8], replicated, may hold values from -0.5 to 0.5
- horizontal_final_matrix: bfloat16 [256, 256], replicated, may hold values from -0.375 to 0.375
- column_query_weight: bfloat16 [256, 256], replicated, as said below
- vertical_attention_matrix: bfloat16 [256, 768], replicated, may hold values from -0.375 to 0.375
- vertical_final_matrix: bfloat16 [256, 256], replicated, may hold values from -0.375 to 0.375
- tensor_mean_lift_matrix: bfloat16 [256, 64], replicated, may hold values from -0.375 to 0.375
- outer_product_output_weight: bfloat16 [1024, 128], replicated, may hold values from -0.75 to 0.75
- triangle_projection_weight: bfloat16 [128, 256], replicated, may hold values from -0.5 to 0.5
- triangle_projection_gate: bfloat16 [128, 256], replicated, may hold values from -0.5 to 0.5
- triangle_output_gate: bfloat16 [128, 128], replicated, may hold values from -0.5 to 0.5
- triangle_output_weight: bfloat16 [128, 128], replicated, may hold values from -0.5 to 0.5
Outputs:
- alignment_output: bfloat16 [512, 128, 256], P('dp', 'axial'), parts along dimension 0
- pair_output: bfloat16 [2048, 128, 128], P(('dp', 'axial')), parts along dimension 0
The draws below stay inside these ranges and needn't reach their ends.
There are 16 independent parts, one for each index of `dp`. The reference program is written for one: setup_inputs(seed, part) draws one part's arguments, and reference() takes and returns one part's arrays. A program takes and returns all parts, laid end to end along the dimension named above; an argument that names none is the same for every part. Nothing has to cross between parts.
Inputs may be any that keep to these rules, and one draw needn't show every extreme that they name: `row_query_weight`: a projection of 256 inputs. `column_query_weight`: a projection of 256 inputs.
All inputs are finite; a program needn't handle non-finite values. No bound on the sum of `pair_valid_mask` on one device may be relied on, other than what follows from the above.
Results may differ from the reference program's by a relative error of at most 0.03.
The reference program's roundings to bfloat16 on the way count: a program that leaves them out, or rounds other values in their place, can miss the bound.
Values may be sent and summed in bfloat16 or wider, within the bound.
A program may use at most 64 MiB of HBM per device.

```python
import jax
import jax.numpy as jnp
from jax import lax

FEATURE_SIZE = 256
C_Z = 128
FOCUS_TOTAL = 8
FOCUS_SIZE = 32
MEAN_HIDDEN_SIZE = 32
C_TRI = 128
SYMBOL_KINDS = 23
LOCAL_SITES = 8
HOMOLOG_TOTAL = 32
SITES_IN_SAMPLE = 128
N_AXIAL = 16


def draw_row_query_weight(key, part):
    key = jax.random.fold_in(key, 11)
    attended_entries = jax.random.normal(key, (FEATURE_SIZE, FOCUS_TOTAL * FOCUS_SIZE), jnp.float32) * FEATURE_SIZE ** (-0.5)
    return attended_entries.astype(jnp.bfloat16)


def draw_column_query_weight(key, part):
    key = jax.random.fold_in(key, 23)
    attended_entries = jax.random.normal(key, (FEATURE_SIZE, FOCUS_TOTAL * FOCUS_SIZE), jnp.float32) * FEATURE_SIZE ** (-0.5)
    return attended_entries.astype(jnp.bfloat16)


def plant(result, rng, least, top_value):
    dims = result.shape
    index_at = [jax.random.randint(jax.random.fold_in(rng, axis), (), 0, dims[axis]) for axis in range(len(dims))]
    result = result.at[tuple(index_at)].set(least)
    longest = dims.index(max(dims))
    index_at[longest] = (index_at[longest] + 1) % dims[longest]
    return result.at[tuple(index_at)].set(top_value)


def levels(own_key, extent, pieces, least, high):
    def one(dim, blocks):
        draws = jax.random.uniform(jax.random.fold_in(jax.random.fold_in(own_key, 6), dim), (blocks,), jnp.float32, least / len(pieces), high / len(pieces))
        return jnp.repeat(jnp.exp(draws), extent[dim] // blocks).reshape((-1,) + (1,) * (len(extent) - dim - 1))

    factor_of = one(*pieces[0])
    for cut in pieces[1:]:
        factor_of = factor_of * one(*cut)
    return factor_of


def bell_draw(key, dims, deviation, bound, shards=(), held_as=jnp.bfloat16):
    level = levels(key, dims, shards, -0.22, 0.18) if shards else 1.0
    values = jax.random.normal(key, dims, jnp.float32) * deviation * level
    return jnp.minimum(jnp.maximum(values, -bound), bound).astype(held_as)


def setup_inputs(seed: int = 0, part: int = 0) -> dict:
    streams_of = jax.random.split(jax.random.key(seed), 20)
    own_keys = jax.random.split(jax.random.fold_in(streams_of[19], part), 20)
    homolog_activity = bell_draw(own_keys[0], (HOMOLOG_TOTAL, SITES_IN_SAMPLE, FEATURE_SIZE), 1.0, 6.0, ((0, 16),))
    homolog_symbol_ids = plant(jax.random.randint(own_keys[1], (HOMOLOG_TOTAL, SITES_IN_SAMPLE), 0, SYMBOL_KINDS), jax.random.fold_in(own_keys[1], 1), 0, SYMBOL_KINDS - 1).astype(jnp.int32)
    residue_present_mask = plant((jax.random.randint(own_keys[2], (SITES_IN_SAMPLE,), 0, 8) < 7).astype(jnp.int32), jax.random.fold_in(own_keys[2], 1), 0, 1)
    pair_state = bell_draw(own_keys[3], (SITES_IN_SAMPLE, SITES_IN_SAMPLE, C_Z), 1.0, 6.0, ((0, 16),))
    pair_valid_mask = plant((jax.random.randint(own_keys[4], (SITES_IN_SAMPLE, SITES_IN_SAMPLE), 0, 8) < 7).astype(jnp.int32), jax.random.fold_in(own_keys[4], 1), 0, 1)
    symbol_lookup_matrix = bell_draw(streams_of[5], (SYMBOL_KINDS, FEATURE_SIZE), 0.5, 3.0)
    row_query_weight = draw_row_query_weight(jax.random.fold_in(streams_of[19], 71), part)
    horizontal_attention_matrix = bell_draw(streams_of[7], (FEATURE_SIZE, 3 * FOCUS_TOTAL * FOCUS_SIZE), FEATURE_SIZE ** -0.5, 0.375)
    pair_bias_weight = bell_draw(streams_of[8], (C_Z, FOCUS_TOTAL), C_Z ** -0.5, 0.5)
    horizontal_final_matrix = bell_draw(streams_of[9], (FOCUS_TOTAL * FOCUS_SIZE, FEATURE_SIZE), (FOCUS_TOTAL * FOCUS_SIZE) ** -0.5, 0.375)
    column_query_weight = draw_column_query_weight(jax.random.fold_in(streams_of[19], 71), part)
    vertical_attention_matrix = bell_draw(streams_of[11], (FEATURE_SIZE, 3 * FOCUS_TOTAL * FOCUS_SIZE), FEATURE_SIZE ** -0.5, 0.375)
    vertical_final_matrix = bell_draw(streams_of[12], (FOCUS_TOTAL * FOCUS_SIZE, FEATURE_SIZE), (FOCUS_TOTAL * FOCUS_SIZE) ** -0.5, 0.375)
    tensor_mean_lift_matrix = bell_draw(streams_of[13], (FEATURE_SIZE, 2 * MEAN_HIDDEN_SIZE), FEATURE_SIZE ** -0.5, 0.375)
    outer_product_output_weight = bell_draw(streams_of[14], (MEAN_HIDDEN_SIZE * MEAN_HIDDEN_SIZE, C_Z), (MEAN_HIDDEN_SIZE * MEAN_HIDDEN_SIZE // 16) ** -0.5, 0.75)
    triangle_projection_weight = bell_draw(streams_of[15], (C_Z, 2 * C_TRI), C_Z ** -0.5, 0.5)
    triangle_projection_gate = bell_draw(streams_of[16], (C_Z, 2 * C_TRI), C_Z ** -0.5, 0.5)
    triangle_output_gate = bell_draw(streams_of[17], (C_Z, C_Z), C_Z ** -0.5, 0.5)
    triangle_output_weight = bell_draw(streams_of[18], (C_TRI, C_Z), C_TRI ** -0.5, 0.5)
    return dict(homolog_activity=homolog_activity, homolog_symbol_ids=homolog_symbol_ids, residue_present_mask=residue_present_mask, pair_state=pair_state, pair_valid_mask=pair_valid_mask, symbol_lookup_matrix=symbol_lookup_matrix, row_query_weight=row_query_weight, horizontal_attention_matrix=horizontal_attention_matrix, pair_bias_weight=pair_bias_weight, horizontal_final_matrix=horizontal_final_matrix, column_query_weight=column_query_weight, vertical_attention_matrix=vertical_attention_matrix, vertical_final_matrix=vertical_final_matrix, tensor_mean_lift_matrix=tensor_mean_lift_matrix, outer_product_output_weight=outer_product_output_weight, triangle_projection_weight=triangle_projection_weight, triangle_projection_gate=triangle_projection_gate, triangle_output_gate=triangle_output_gate, triangle_output_weight=triangle_output_weight)


def layer_normalize(attended_entries):
    attended_entries = attended_entries.astype(jnp.float32)
    mean = lax.optimization_barrier(jnp.mean(attended_entries, axis=-1, keepdims=True))
    centred = attended_entries - mean
    var = lax.optimization_barrier(jnp.mean(centred * centred, axis=-1, keepdims=True))
    return centred * lax.rsqrt(var + 1e-05)

def gated_attend(evoformer_block, extra_axes, w_query, w_kvg, w_out):
    lines_list, residue_length, input_width = evoformer_block.shape
    width = FOCUS_TOTAL * FOCUS_SIZE
    flat = layer_normalize(evoformer_block).astype(jnp.bfloat16).reshape(lines_list * residue_length, input_width)
    query = (jnp.dot(flat, w_query, preferred_element_type=jnp.float32) * FOCUS_SIZE ** (-0.5)).astype(jnp.bfloat16)
    query = query.reshape(lines_list, residue_length, FOCUS_TOTAL, FOCUS_SIZE)
    kvg = jnp.dot(flat, w_kvg, preferred_element_type=jnp.float32)
    keys = kvg[:, :width].astype(jnp.bfloat16).reshape(lines_list, residue_length, FOCUS_TOTAL, FOCUS_SIZE)
    attended_entries = kvg[:, width:2 * width].astype(jnp.bfloat16).reshape(lines_list, residue_length, FOCUS_TOTAL, FOCUS_SIZE)
    gate = jax.nn.sigmoid(kvg[:, 2 * width:]).reshape(lines_list, residue_length, FOCUS_TOTAL, FOCUS_SIZE)
    scores = jnp.einsum('bihd,bjhd->bhij', query.astype(jnp.float32), keys.astype(jnp.float32)) + extra_axes
    top = lax.optimization_barrier(jnp.max(scores, axis=-1, keepdims=True))
    expo = jnp.exp(scores - top)
    weights = (expo / lax.optimization_barrier(jnp.sum(expo, axis=-1, keepdims=True))).astype(jnp.bfloat16)
    mixed = jnp.einsum('bhij,bjhd->bihd', weights.astype(jnp.float32), attended_entries.astype(jnp.float32))
    mixed = (mixed * gate).astype(jnp.bfloat16).reshape(lines_list * residue_length, width)
    return evoformer_block + jnp.dot(mixed, w_out, preferred_element_type=jnp.float32).reshape(lines_list, residue_length, input_width)

def reference(homolog_activity, homolog_symbol_ids, residue_present_mask, pair_state, pair_valid_mask, symbol_lookup_matrix, row_query_weight, horizontal_attention_matrix, pair_bias_weight, horizontal_final_matrix, column_query_weight, vertical_attention_matrix, vertical_final_matrix, tensor_mean_lift_matrix, outer_product_output_weight, triangle_projection_weight, triangle_projection_gate, triangle_output_gate, triangle_output_weight):
    homolog_starting = homolog_activity.astype(jnp.float32) + symbol_lookup_matrix.astype(jnp.float32)[homolog_symbol_ids]
    pair_norm = layer_normalize(pair_state).astype(jnp.bfloat16)
    bias = jnp.dot(pair_norm.reshape(SITES_IN_SAMPLE * SITES_IN_SAMPLE, C_Z), pair_bias_weight, preferred_element_type=jnp.float32)
    bias = jnp.transpose(bias.astype(jnp.bfloat16).reshape(SITES_IN_SAMPLE, SITES_IN_SAMPLE, FOCUS_TOTAL), (2, 0, 1)).astype(jnp.float32)
    key_bias = 1000000000.0 * (residue_present_mask.astype(jnp.float32) - 1.0)
    extra_axes = bias[None] + key_bias[None, None, None, :]
    cluster_total = homolog_starting.reshape(HOMOLOG_TOTAL // 2, 2, SITES_IN_SAMPLE, FEATURE_SIZE)
    homolog_across_update = lax.map(lambda evoformer_block: gated_attend(evoformer_block, extra_axes, row_query_weight, horizontal_attention_matrix, horizontal_final_matrix), cluster_total)
    homolog_across_update = homolog_across_update.reshape(HOMOLOG_TOTAL, SITES_IN_SAMPLE, FEATURE_SIZE).astype(jnp.bfloat16)
    column_count = jnp.swapaxes(homolog_across_update, 0, 1)
    column_finished = lax.map(lambda item: gated_attend(item[None].astype(jnp.float32), 0.0, column_query_weight, vertical_attention_matrix, vertical_final_matrix)[0], column_count)
    alignment_output = jnp.swapaxes(column_finished, 0, 1).astype(jnp.bfloat16)
    tensor_mean_scaler = layer_normalize(alignment_output).astype(jnp.bfloat16)
    split_parts = jnp.dot(tensor_mean_scaler.reshape(HOMOLOG_TOTAL * SITES_IN_SAMPLE, FEATURE_SIZE), tensor_mean_lift_matrix, preferred_element_type=jnp.float32)
    split_parts = split_parts.astype(jnp.bfloat16).reshape(HOMOLOG_TOTAL, SITES_IN_SAMPLE, 2 * MEAN_HIDDEN_SIZE)
    first_factor = split_parts[..., :MEAN_HIDDEN_SIZE].astype(jnp.float32)
    second_factor = split_parts[..., MEAN_HIDDEN_SIZE:].astype(jnp.float32)
    first_factor_lines = jnp.swapaxes(first_factor, 0, 1).reshape(N_AXIAL, LOCAL_SITES, HOMOLOG_TOTAL, MEAN_HIDDEN_SIZE)

    def opm_block(lines_list):
        tensor_mean = jnp.einsum('kxh,xgo->kgho', lines_list, second_factor) / HOMOLOG_TOTAL
        tensor_mean = tensor_mean.reshape(LOCAL_SITES * SITES_IN_SAMPLE, MEAN_HIDDEN_SIZE * MEAN_HIDDEN_SIZE).astype(jnp.bfloat16)
        return jnp.dot(tensor_mean, outer_product_output_weight, preferred_element_type=jnp.float32).reshape(LOCAL_SITES, SITES_IN_SAMPLE, C_Z)
    update = lax.map(opm_block, first_factor_lines).reshape(SITES_IN_SAMPLE, SITES_IN_SAMPLE, C_Z)
    pair_one = pair_state.astype(jnp.float32) + update
    tri_norm = layer_normalize(pair_one).astype(jnp.bfloat16)
    flat = tri_norm.reshape(SITES_IN_SAMPLE * SITES_IN_SAMPLE, C_Z)
    proj = jnp.dot(flat, triangle_projection_weight, preferred_element_type=jnp.float32)
    gates = jnp.dot(flat, triangle_projection_gate, preferred_element_type=jnp.float32)
    both = (jax.nn.sigmoid(gates) * proj * pair_valid_mask.astype(jnp.float32).reshape(SITES_IN_SAMPLE * SITES_IN_SAMPLE, 1)).astype(jnp.bfloat16)
    both = both.reshape(SITES_IN_SAMPLE, SITES_IN_SAMPLE, 2 * C_TRI)
    left_tri = jnp.transpose(both[..., :C_TRI], (2, 0, 1)).astype(jnp.float32)
    right_tri = jnp.transpose(both[..., C_TRI:], (2, 0, 1)).astype(jnp.float32)
    tri_sum = jnp.einsum('cik,cjk->cij', left_tri, right_tri)
    tri_mixed = layer_normalize(jnp.transpose(tri_sum, (1, 2, 0))).astype(jnp.bfloat16)
    tri_update = jnp.dot(tri_mixed.reshape(SITES_IN_SAMPLE * SITES_IN_SAMPLE, C_TRI), triangle_output_weight, preferred_element_type=jnp.float32).reshape(SITES_IN_SAMPLE, SITES_IN_SAMPLE, C_Z)
    out_gate = jax.nn.sigmoid(jnp.dot(flat, triangle_output_gate, preferred_element_type=jnp.float32)).reshape(SITES_IN_SAMPLE, SITES_IN_SAMPLE, C_Z)
    pair_output = (pair_one + out_gate * tri_update).astype(jnp.bfloat16)
    return (alignment_output, pair_output)
```

```python
import jax
import jax.numpy as jnp
from jax import lax
from jax.experimental import pallas as pl
from jax.experimental.pallas import tpu as pltpu
from jax.sharding import PartitionSpec as P

N = 16
HEADS = 8
HEAD = 32
F32 = jnp.float32
BF16 = jnp.bfloat16
NN = (((1,), (0,)), ((), ()))
NT = (((1,), (1,)), ((), ()))
TN = (((0,), (0,)), ((), ()))

BIAS, MSA, OPM, TRI, SUM = range(5)


def dot(a, b, dims=NN):
    return lax.dot_general(a, b, dims, preferred_element_type=F32)


def sigmoid(x):
    return 1.0 / (1.0 + jnp.exp(-x))


def norm(x, axis=-1):
    centred = x - jnp.mean(x, axis=axis, keepdims=True)
    var = jnp.mean(centred * centred, axis=axis, keepdims=True)
    return (centred * lax.rsqrt(var + 1e-05)).astype(BF16)


def kernel(
    act, ids, present, pair, valid, table,
    row_q, row_kvg, bias_w, row_o, col_q, col_kvg, col_o,
    lift, opm_w, tri_w, tri_g, out_g, out_w,
    msa_out, pair_out,
    bias_send, bias_recv, msa_send, msa_recv, opm_send, opm_recv,
    tri_send, tri_recv, sum_send, sum_recv,
    bias_rows, bias_all, table_pad, xr, w2, wt, lift_x, opm_f, tcat,
    pair_one, tri_n, gate, xt, yt, zt,
    send_sem, recv_sem,
):
    me = lax.axis_index("axial")
    barrier = pltpu.get_barrier_semaphore()
    for r in range(1, N):
        pl.semaphore_signal(
            barrier, inc=1, device_id={"axial": lax.rem(me + r, N)},
            device_id_type=pl.DeviceIdType.MESH,
        )

    def copy(phase, r, src, dst):
        return pltpu.make_async_remote_copy(
            src_ref=src, dst_ref=dst,
            send_sem=send_sem.at[phase, r], recv_sem=recv_sem.at[phase, r],
            device_id={"axial": lax.rem(me + r, N)},
            device_id_type=pl.DeviceIdType.MESH,
        )

    def gather_copy(phase, r, send, recv):
        return copy(phase, r, send, recv.at[me])

    def scatter_copy(phase, r, send, recv):
        return copy(phase, r, send.at[lax.rem(me + r, N)], recv.at[me])

    def await_all(phase, recv):
        for r in range(1, N):
            src = lax.rem(me + (N - r), N)
            pltpu.make_async_remote_copy(
                src_ref=recv.at[src], dst_ref=recv.at[src],
                send_sem=send_sem.at[phase, r], recv_sem=recv_sem.at[phase, r],
                device_id={"axial": lax.rem(me + r, N)},
                device_id_type=pl.DeviceIdType.MESH,
            ).wait_recv()

    pn = norm(pair[...].astype(F32)).reshape(1024, 128)
    bias_t = dot(bias_w[...].astype(F32).T.astype(BF16), pn, NT)
    for i in range(8):
        bias_rows[pl.ds(i, 8, stride=8), :] = bias_t[:, i * 128:(i + 1) * 128]
    bias_send[...] = bias_rows[...].astype(BF16)
    bias_recv[me] = bias_rows[...].astype(BF16)

    pl.semaphore_wait(barrier, N - 1)
    for r in range(1, N):
        gather_copy(BIAS, r, bias_send, bias_recv).start()

    table_pad[...] = jnp.zeros((32, 256), F32)
    table_pad[0:23, :] = table[...].astype(F32)
    table_b = table_pad[...].astype(BF16)
    kinds = lax.broadcasted_iota(jnp.int32, (32, 128), 0)
    x_rows = []
    for s in range(2):
        hot = (kinds == ids[s:s + 1, :]).astype(F32).T.astype(BF16)
        x_rows.append(act[s].astype(F32) + dot(hot, table_b))
    x = jnp.concatenate(x_rows, axis=0)

    head_of = lax.broadcasted_iota(jnp.int32, (1, 256), 1) // HEAD
    head_mask = [(head_of == h).astype(F32).astype(BF16) for h in range(HEADS)]

    def project(x, wq, wkvg):
        xn = norm(x)
        q = (dot(xn, wq[...]) * HEAD ** -0.5).astype(BF16)
        kvg = dot(xn, wkvg[...])
        return q, kvg[:, :256].astype(BF16), kvg[:, 256:512].astype(BF16), kvg[:, 512:]

    def attend(q, k, v, g, extra):
        halves = []
        for s in range(2):
            rows = slice(s * 128, (s + 1) * 128)
            acc = jnp.zeros((128, 256), F32)
            for h in range(HEADS):
                scores = dot(q[rows] * head_mask[h], k[rows], NT) + extra(h)
                top = jnp.max(scores, axis=-1, keepdims=True)
                expo = jnp.exp(scores - top)
                total = jnp.sum(expo, axis=-1, keepdims=True)
                weights = (expo * (1.0 / total)).astype(BF16)
                mixed = dot(weights, v[rows])
                acc = jnp.where(head_of == h, mixed, acc)
            halves.append(acc)
        return (jnp.concatenate(halves, axis=0) * sigmoid(g)).astype(BF16)

    q, k, v, g = project(x, row_q, row_kvg)

    opm_f[...] = opm_w[...].astype(F32)
    for d in range(32):
        w2[:, d * 128:(d + 1) * 128] = opm_f[pl.ds(d, 32, stride=32), :].astype(BF16)
    wt[0:256, :] = tri_w[...].astype(F32).T.astype(BF16)
    wt[256:512, :] = tri_g[...].astype(F32).T.astype(BF16)
    spread = (
        lax.broadcasted_iota(jnp.int32, (64, 1024), 0)
        == 32 + lax.broadcasted_iota(jnp.int32, (64, 1024), 1) // 32
    ).astype(F32).astype(BF16)
    lift_x[...] = dot(lift[...], spread).astype(BF16)

    await_all(BIAS, bias_recv)
    key_bias = 1000000000.0 * (present[...].astype(F32) - 1.0)
    for p in range(N):
        block = bias_recv[p].astype(F32)
        for h in range(HEADS):
            bias_all[h, p * 8:(p + 1) * 8, :] = block[h * 8:(h + 1) * 8] + key_bias
    heads = attend(q, k, v, g, lambda h: bias_all[h])
    msa_one = x + dot(heads, row_o[...])
    for p in range(N):
        block = jnp.concatenate(
            [msa_one[p * 8:(p + 1) * 8], msa_one[128 + p * 8:128 + (p + 1) * 8]], axis=0
        )
        msa_send[p] = block.astype(BF16)
    msa_recv[me] = msa_send[me]
    for r in range(1, N):
        scatter_copy(MSA, r, msa_send, msa_recv).start()
    await_all(MSA, msa_recv)

    for p in range(N):
        block = msa_recv[p].astype(F32)
        for half in range(2):
            xr[half, p * 16:(p + 1) * 16, :] = block[:, half * 128:(half + 1) * 128]
    x = jnp.concatenate(
        [
            jnp.concatenate(
                [xr[half, pl.ds(l, 32, stride=8), :] for l in range(8)], axis=0
            )
            for half in range(2)
        ],
        axis=1,
    )
    q, k, v, g = project(x, col_q, col_kvg)
    own = jnp.where(
        lax.broadcasted_iota(jnp.int32, (128, 128), 0) // 32
        == lax.broadcasted_iota(jnp.int32, (128, 128), 1) // 32,
        0.0, -jnp.inf,
    ).astype(F32)
    heads = attend(q, k, v, g, lambda h: own)
    z = (x + dot(heads, col_o[...])).astype(BF16)

    zf = z.astype(F32)
    zn = norm(zf)
    right = dot(zn, lift_x[...])
    keep = (
        lax.broadcasted_iota(jnp.int32, (256, 1024), 0) % 32
        == lax.broadcasted_iota(jnp.int32, (256, 1024), 1) % 32
    )
    right = jnp.where(keep, right, 0.0).astype(BF16)
    pick = (
        lax.broadcasted_iota(jnp.int32, (8, 256), 0)
        == lax.broadcasted_iota(jnp.int32, (8, 256), 1) // 32
    ).astype(F32).astype(BF16)
    right = dot(pick, right)
    right = jnp.concatenate([right[:, :512], right[:, 512:]], axis=0).astype(BF16)
    opm_send[...] = right
    opm_recv[me] = right
    for r in range(1, N):
        gather_copy(OPM, r, opm_send, opm_recv).start()

    for half in range(2):
        for l in range(8):
            xr[half, pl.ds(l, 32, stride=8), :] = zf[
                l * 32:(l + 1) * 32, half * 128:(half + 1) * 128
            ]
    for half in range(2):
        msa_out[:, :, half * 128:(half + 1) * 128] = (
            xr[half].reshape(32, 8, 128).astype(BF16)
        )
    left = dot(zn, lift[...]).astype(BF16)[:, :32]
    for d in range(0, 32, 2):
        t = dot(left, w2[:, d * 128:(d + 2) * 128]).astype(BF16)
        for i in range(8):
            for e in range(2):
                tcat[(d + e) * 32:(d + e + 1) * 32, i * 128:(i + 1) * 128] = t[
                    i * 32:(i + 1) * 32, e * 128:(e + 1) * 128
                ]

    await_all(OPM, opm_recv)
    blocks = [opm_recv[p].astype(F32) for p in range(N)]
    right = jnp.concatenate(
        [
            jnp.concatenate([b[:8] for b in blocks], axis=0),
            jnp.concatenate([b[8:] for b in blocks], axis=0),
        ],
        axis=1,
    ).astype(BF16)

    for i in range(8):
        update = dot(right, tcat[:, i * 128:(i + 1) * 128])
        one = pair[i].astype(F32) + update * (1.0 / 32)
        pair_one[i] = one
        tn = norm(one)
        tri_n[i] = tn
        both = dot(wt[...], tn, NT)
        both = sigmoid(both[256:]) * both[:256] * valid[i:i + 1, :].astype(F32)
        for p in range(N):
            block = jnp.concatenate(
                [both[p * 8:(p + 1) * 8], both[128 + p * 8:128 + (p + 1) * 8]], axis=0
            )
            tri_send[p, :, i * 128:(i + 1) * 128] = block.astype(BF16)
    tri_recv[me] = tri_send[me]
    for r in range(1, N):
        scatter_copy(TRI, r, tri_send, tri_recv).start()
    for i in range(8):
        gate[i] = sigmoid(dot(tri_n[i], out_g[...]))
    await_all(TRI, tri_recv)

    for p in range(N):
        for i in range(8):
            at = (p * 8 + i) * 16
            xt[at:at + 16, :] = tri_recv[p, :, i * 128:(i + 1) * 128].astype(F32)
    for c in range(8):
        a = xt[pl.ds(c, 128, stride=16), :].astype(BF16)
        b = xt[pl.ds(8 + c, 128, stride=16), :].astype(BF16)
        yt[pl.ds(c, 128, stride=8), :] = dot(a, b, NT)
    for p in range(N):
        sum_send[p] = yt[p * 64:(p + 1) * 64, :].astype(BF16)
    sum_recv[me] = sum_send[me]
    for r in range(1, N):
        scatter_copy(SUM, r, sum_send, sum_recv).start()
    await_all(SUM, sum_recv)

    for p in range(N):
        block = sum_recv[p].astype(F32)
        for i in range(8):
            zt[i, p * 8:(p + 1) * 8, :] = block[i * 8:(i + 1) * 8]
    for i in range(8):
        mixed = norm(zt[i], axis=0)
        update = dot(mixed, out_w[...], TN)
        pair_out[i] = (pair_one[i] + gate[i] * update).astype(BF16)

    for r in range(1, N):
        gather_copy(BIAS, r, bias_send, bias_recv).wait_send()
        scatter_copy(MSA, r, msa_send, msa_recv).wait_send()
        gather_copy(OPM, r, opm_send, opm_recv).wait_send()
        scatter_copy(TRI, r, tri_send, tri_recv).wait_send()
        scatter_copy(SUM, r, sum_send, sum_recv).wait_send()


def local(act, ids, present, *rest):
    vmem = pl.BlockSpec(memory_space=pltpu.VMEM)
    args = (act, ids, present.reshape(1, 128), *rest)
    return pl.pallas_call(
        kernel,
        out_shape=(
            jax.ShapeDtypeStruct((32, 8, 256), BF16),
            jax.ShapeDtypeStruct((8, 128, 128), BF16),
        ),
        in_specs=[vmem] * len(args),
        out_specs=(vmem, vmem),
        scratch_shapes=[
            pltpu.VMEM((64, 128), BF16),
            pltpu.VMEM((N, 64, 128), BF16),
            pltpu.VMEM((N, 16, 256), BF16),
            pltpu.VMEM((N, 16, 256), BF16),
            pltpu.VMEM((16, 512), BF16),
            pltpu.VMEM((N, 16, 512), BF16),
            pltpu.VMEM((N, 16, 1024), BF16),
            pltpu.VMEM((N, 16, 1024), BF16),
            pltpu.VMEM((N, 64, 128), BF16),
            pltpu.VMEM((N, 64, 128), BF16),
            pltpu.VMEM((64, 128), F32),
            pltpu.VMEM((HEADS, 128, 128), F32),
            pltpu.VMEM((32, 256), F32),
            pltpu.VMEM((2, 256, 128), F32),
            pltpu.VMEM((32, 4096), BF16),
            pltpu.VMEM((512, 128), BF16),
            pltpu.VMEM((256, 1024), BF16),
            pltpu.VMEM((1024, 128), F32),
            pltpu.VMEM((1024, 1024), BF16),
            pltpu.VMEM((8, 128, 128), F32),
            pltpu.VMEM((8, 128, 128), BF16),
            pltpu.VMEM((8, 128, 128), F32),
            pltpu.VMEM((2048, 128), F32),
            pltpu.VMEM((1024, 128), F32),
            pltpu.VMEM((8, 128, 128), F32),
            pltpu.SemaphoreType.DMA((5, N)),
            pltpu.SemaphoreType.DMA((5, N)),
        ],
        compiler_params=pltpu.CompilerParams(
            collective_id=0, has_side_effects=True, vmem_limit_bytes=48 * 1024 * 1024,
        ),
        cost_estimate=pl.CostEstimate(flops=10**9, bytes_accessed=3 * 10**6, transcendentals=10**6),
    )(*args)


def solution(mesh):
    rows = P(("dp", "axial"))
    return jax.shard_map(
        local,
        mesh=mesh,
        in_specs=(rows, rows, P("dp"), rows, rows) + (P(),) * 14,
        out_specs=(P("dp", "axial", None), rows),
        check_vma=False,
    )
```

```python
import jax
import jax.numpy as jnp
from jax import lax
from jax.experimental import pallas as pl
from jax.experimental.pallas import tpu as pltpu
from jax.sharding import PartitionSpec as P

N = 16
HEADS = 8
HEAD = 32
INPUTS = 19
F32 = jnp.float32
BF16 = jnp.bfloat16
NN = (((1,), (0,)), ((), ()))
NT = (((1,), (1,)), ((), ()))
TN = (((0,), (0,)), ((), ()))
MESH = pl.DeviceIdType.MESH
OFFSETS = (1, 15, 2, 14, 3, 13, 4, 12, 5, 11, 6, 10, 7, 9, 8)
BIAS, MSA, OPM, TRI, SUM, WIRES = 0, 1, 2, 4, 6, 7


def dot(a, b, dims=NN):
    return lax.dot_general(a, b, dims, preferred_element_type=F32)


def sigmoid(x):
    return 0.5 * jnp.tanh(0.5 * x) + 0.5


def norm(x, axis=-1):
    centred = x - jnp.mean(x, axis=axis, keepdims=True)
    var = jnp.mean(centred * centred, axis=axis, keepdims=True)
    return (centred * lax.rsqrt(var + 1e-05)).astype(BF16)


def iota(shape, axis):
    return lax.broadcasted_iota(jnp.int32, shape, axis)


def ones_where(condition):
    return condition.astype(F32).astype(BF16)


def kernel(*refs):
    n = INPUTS
    body(refs[:n], refs[n], refs[n + 1], refs[n + 2:2 * n + 2], *refs[2 * n + 2:])


def body(
    hbm, msa_out, pair_out, held,
    bias_send, bias_recv, msa_send, msa_recv, opm_send, opm_recv,
    tri_send, tri_recv, sum_send, sum_recv,
    bias_rows, bias_all, table_pad, score, head_ones, xr, w2, wt, lift_x, opm_f, tcat,
    right_f, pair_one, tri_n, gate, xt, zt,
    in_sem, send_sem, recv_sem,
):
    (
        act, ids, present, pair, valid, table,
        row_q, row_kvg, bias_w, row_o, col_q, col_kvg, col_o,
        lift, opm_w, tri_w, tri_g, out_g, out_w,
    ) = held
    loads = {
        id(to): pltpu.make_async_copy(at, to, in_sem.at[n])
        for n, (at, to) in enumerate(zip(hbm, held))
    }
    for ref in (pair, bias_w):
        loads[id(ref)].start()

    me = lax.axis_index("axial")
    peers = {r: lax.rem(me + r, N) for r in OFFSETS}
    barrier = pltpu.get_barrier_semaphore()
    for r in OFFSETS:
        pl.semaphore_signal(
            barrier, inc=1, device_id={"axial": peers[r]}, device_id_type=MESH
        )
    for ref in (
        ids, act, table, row_q, row_kvg, present, row_o, opm_w, lift,
        tri_w, tri_g, col_q, col_kvg, col_o, valid, out_g, out_w,
    ):
        loads[id(ref)].start()

    def need(*refs):
        for ref in refs:
            loads.pop(id(ref)).wait()

    wires = {BIAS: (bias_send, bias_recv)}
    for s in range(1):
        wires[MSA + s] = (msa_send.at[s], msa_recv.at[s])
    for s in range(2):
        wires[OPM + s] = (opm_send.at[s], opm_recv.at[s])
    for s in range(2):
        wires[TRI + s] = (tri_send.at[s], tri_recv.at[s])
    for s in range(1):
        wires[SUM + s] = (sum_send.at[s], sum_recv.at[s])

    def copy(wire, r, src, dst):
        return pltpu.make_async_remote_copy(
            src_ref=src, dst_ref=dst,
            send_sem=send_sem.at[wire], recv_sem=recv_sem.at[wire],
            device_id={"axial": peers[r]}, device_id_type=MESH,
        )

    def outgoing(wire):
        src, dst = wires[wire]
        whole = wire == BIAS or OPM <= wire < TRI
        return [
            copy(wire, r, src if whole else src.at[peers[r]], dst.at[me])
            for r in OFFSETS
        ]

    def send(wire):
        src, dst = wires[wire]
        for c in outgoing(wire):
            c.start()
        whole = wire == BIAS or OPM <= wire < TRI
        dst[me] = src[...] if whole else src[me]

    def finish(wire):
        at = wires[wire][1].at[pl.ds(0, N - 1)]
        copy(wire, 1, at, at).wait_send()

    def await_all(wire):
        at = wires[wire][1].at[pl.ds(0, N - 1)]
        copy(wire, 1, at, at).wait_recv()

    need(pair, bias_w)
    pn = norm(pair[...].astype(F32)).reshape(1024, 128)
    bias_t = dot(bias_w[...], pn, NT)
    for i in range(8):
        bias_rows[pl.ds(i, 8, stride=8), :] = bias_t[:, i * 128:(i + 1) * 128]
    bias_send[...] = bias_rows[...].astype(BF16)
    pl.semaphore_wait(barrier, N - 1)
    send(BIAS)

    need(table, ids, act, row_q, row_kvg)
    head_of = iota((1, 256), 1) // HEAD
    head_mask = [ones_where(head_of == h) for h in range(HEADS)]

    def project(x, wq, wkvg):
        xn = norm(x)
        q = (dot(xn, wq[...]) * HEAD ** -0.5).astype(BF16)
        kvg = dot(xn, wkvg[...])
        return q, kvg[:, :256].astype(BF16), kvg[:, 256:512].astype(BF16), kvg[:, 512:]

    def by_head(a):
        return jnp.concatenate([a * m for m in head_mask], axis=0)

    def mix(scores, extra, v, g):
        parts = []
        for h in range(HEADS):
            one = scores[h * 128:(h + 1) * 128] + extra(h)
            parts.append(jnp.exp(one - jnp.max(one, axis=-1, keepdims=True)).astype(BF16))
        weights = jnp.concatenate(parts, axis=1)
        total = dot(weights, head_ones[...])
        return (dot(weights, by_head(v)) * (sigmoid(g) / total)).astype(BF16)

    table_pad[...] = jnp.zeros((32, 256), F32)
    table_pad[0:23, :] = table[...].astype(F32)
    table_b = table_pad[...].astype(BF16)
    rows = []
    for s in range(2):
        hot = (iota((32, 128), 0) == ids[s:s + 1, :]).astype(F32).T.astype(BF16)
        x = act[s].astype(F32) + dot(hot, table_b)
        q, k, v, g = project(x, row_q, row_kvg)
        score[s] = dot(by_head(q), k, NT)
        rows.append((x, v, g))

    head_ones[...] = ones_where(iota((1024, 256), 0) // 128 == iota((1024, 256), 1) // HEAD)
    need(opm_w, lift, tri_w, tri_g)
    opm_f[...] = opm_w[...].astype(F32)
    for d in range(32):
        w2[:, d * 128:(d + 1) * 128] = opm_f[pl.ds(d, 32, stride=32), :].astype(BF16)
    wt[0:256, :] = tri_w[...].astype(F32).T.astype(BF16)
    wt[256:512, :] = tri_g[...].astype(F32).T.astype(BF16)
    spread = ones_where(iota((64, 1024), 0) == 32 + iota((64, 1024), 1) // 32)
    lift_x[...] = dot(lift[...], spread, TN).astype(BF16)

    need(present, row_o, col_q, col_kvg, col_o, valid, out_g, out_w)
    await_all(BIAS)
    key_bias = 1000000000.0 * (present[...].astype(F32) - 1.0)
    for p in range(N):
        block = bias_recv[p].astype(F32)
        for h in range(HEADS):
            bias_all[h, p * 8:(p + 1) * 8, :] = block[h * 8:(h + 1) * 8] + key_bias
    for s in range(2):
        x, v, g = rows[s]
        heads = mix(score[s], lambda h: bias_all[h], v, g)
        x = x + dot(heads, row_o[...])
        for p in range(N):
            block = x[p * 8:(p + 1) * 8]
            msa_send[0, p, s * 16:(s + 1) * 16, :] = jnp.concatenate([block[:, :128], block[:, 128:]], axis=0).astype(BF16)

    send(MSA)

    await_all(MSA)
    for p in range(N):
        block = msa_recv[0, p].astype(F32)
        for s in range(2):
            at = (p * 2 + s) * 8
            for half in range(2):
                xr[half, at:at + 8, :] = block[(s * 2 + half) * 8:(s * 2 + half + 1) * 8]

    own = jnp.where(iota((128, 128), 0) // 32 == iota((128, 128), 1) // 32, 0.0, -jnp.inf)
    own = own.astype(F32)
    keep = iota((128, 1024), 0) % 32 == iota((128, 1024), 1) % 32
    done = []
    for n in range(2):
        x = jnp.concatenate(
            [
                jnp.concatenate(
                    [xr[half, pl.ds(n * 4 + l, 32, stride=8), :] for l in range(4)], axis=0
                )
                for half in range(2)
            ],
            axis=1,
        )
        q, k, v, g = project(x, col_q, col_kvg)
        heads = mix(dot(by_head(q), k, NT), lambda h: own, v, g)
        z = (x + dot(heads, col_o[...])).astype(BF16).astype(F32)
        zn = norm(z)
        right = dot(zn, lift_x[...])
        right = jnp.where(keep, right, 0.0).astype(BF16)
        total = jnp.zeros((16, 256), F32)
        for a in range(4):
            pick = ones_where(iota((16, 128), 0) == a * 4 + iota((16, 128), 1) // 32)
            total += dot(pick, right[:, a * 256:(a + 1) * 256])
        opm_send[n] = total.astype(BF16)
        send(OPM + n)
        done.append((z, zn))

    for n in range(2):
        z = done[n][0]
        for half in range(2):
            for l in range(4):
                xr[half, pl.ds(n * 4 + l, 32, stride=8), :] = z[
                    l * 32:(l + 1) * 32, half * 128:(half + 1) * 128
                ]
    for half in range(2):
        msa_out[:, :, half * 128:(half + 1) * 128] = xr[half].reshape(32, 8, 128).astype(BF16)
    zn = jnp.concatenate([done[0][1], done[1][1]], axis=0)
    left = dot(zn, lift[0:32, :], NT).astype(BF16)
    for d in range(0, 32, 2):
        t = dot(left, w2[:, d * 128:(d + 2) * 128]).astype(BF16)
        for i in range(8):
            for e in range(2):
                tcat[(d + e) * 32:(d + e + 1) * 32, i * 128:(i + 1) * 128] = t[
                    i * 32:(i + 1) * 32, e * 128:(e + 1) * 128
                ]

    for n in range(2):
        await_all(OPM + n)
        for p in range(N):
            block = opm_recv[n, p].astype(F32)
            at = p * 8 + n * 4
            for a in range(4):
                right_f[at:at + 4, a * 256:(a + 1) * 256] = block[a * 4:(a + 1) * 4]
    right = right_f[...].astype(BF16)

    for n in range(4):
        update = dot(right, tcat[:, n * 256:(n + 1) * 256])
        for e in range(2):
            i = n * 2 + e
            one = pair[i].astype(F32) + update[:, e * 128:(e + 1) * 128] * (1.0 / 32)
            pair_one[i] = one
            tn = norm(one)
            tri_n[i] = tn
            both = dot(wt[...], tn, NT)
            both = sigmoid(both[256:]) * both[:256] * valid[i:i + 1, :].astype(F32)
            for p in range(N):
                block = jnp.concatenate(
                    [both[p * 8:(p + 1) * 8], both[128 + p * 8:128 + (p + 1) * 8]], axis=0
                )
                tri_send[n // 2, p, :, (n % 2 * 2 + e) * 128:(n % 2 * 2 + e + 1) * 128] = block.astype(BF16)
        if n % 2 == 1:
            send(TRI + n // 2)
    for i in range(8):
        gate[i] = sigmoid(dot(tri_n[i], out_g[...]))
    for n in range(2):
        await_all(TRI + n)
        for p in range(N):
            block = tri_recv[n, p].astype(F32)
            for e in range(4):
                at = (p * 8 + n * 4 + e) * 16
                xt[at:at + 16, :] = block[:, e * 128:(e + 1) * 128]

    for n in range(1):
        sums = []
        for c in range(n * 8, (n + 1) * 8):
            a = xt[pl.ds(c, 128, stride=16), :].astype(BF16)
            b = xt[pl.ds(8 + c, 128, stride=16), :].astype(BF16)
            sums.append(dot(a, b, NT))
        for p in range(N):
            sum_send[n, p] = jnp.concatenate(
                [s[p * 8:(p + 1) * 8] for s in sums], axis=0
            ).astype(BF16)
        send(SUM + n)
    for n in range(1):
        await_all(SUM + n)
        for p in range(N):
            at = (p * 8 + n * 8) * 8
            zt[at:at + 64, :] = sum_recv[n, p].astype(F32)

    for i in range(8):
        mixed = norm(zt[pl.ds(i, 128, stride=8), :], axis=0)
        update = dot(mixed, out_w[...], TN)
        pair_out[i] = (pair_one[i] + gate[i] * update).astype(BF16)
    for wire in wires:
        finish(wire)


def local(*args):
    hbm = pl.BlockSpec(memory_space=pl.ANY)
    vmem = pl.BlockSpec(memory_space=pltpu.VMEM)
    args = list(args)
    args[2] = args[2].reshape(1, 128)
    args[8] = args[8].T
    args[13] = args[13].T
    shapes = (
        jax.ShapeDtypeStruct((32, 8, 256), BF16),
        jax.ShapeDtypeStruct((8, 128, 128), BF16),
    )
    return pl.pallas_call(
        kernel,
        out_shape=shapes,
        in_specs=[hbm] * len(args),
        out_specs=(vmem, vmem),
        scratch_shapes=[pltpu.VMEM(a.shape, a.dtype) for a in args] + [
            pltpu.VMEM((64, 128), BF16),
            pltpu.VMEM((N, 64, 128), BF16),
            pltpu.VMEM((1, N, 32, 128), BF16),
            pltpu.VMEM((1, N, 32, 128), BF16),
            pltpu.VMEM((2, 16, 256), BF16),
            pltpu.VMEM((2, N, 16, 256), BF16),
            pltpu.VMEM((2, N, 16, 512), BF16),
            pltpu.VMEM((2, N, 16, 512), BF16),
            pltpu.VMEM((1, N, 64, 128), BF16),
            pltpu.VMEM((1, N, 64, 128), BF16),
            pltpu.VMEM((64, 128), F32),
            pltpu.VMEM((HEADS, 128, 128), F32),
            pltpu.VMEM((32, 256), F32),
            pltpu.VMEM((2, 1024, 128), F32),
            pltpu.VMEM((1024, 256), BF16),
            pltpu.VMEM((2, 256, 128), F32),
            pltpu.VMEM((32, 4096), BF16),
            pltpu.VMEM((512, 128), BF16),
            pltpu.VMEM((256, 1024), BF16),
            pltpu.VMEM((1024, 128), F32),
            pltpu.VMEM((1024, 1024), BF16),
            pltpu.VMEM((128, 1024), F32),
            pltpu.VMEM((8, 128, 128), F32),
            pltpu.VMEM((8, 128, 128), BF16),
            pltpu.VMEM((8, 128, 128), F32),
            pltpu.VMEM((2048, 128), F32),
            pltpu.VMEM((1024, 128), F32),
            pltpu.SemaphoreType.DMA((INPUTS,)),
            pltpu.SemaphoreType.DMA((WIRES,)),
            pltpu.SemaphoreType.DMA((WIRES,)),
        ],
        compiler_params=pltpu.CompilerParams(
            collective_id=0, has_side_effects=True, vmem_limit_bytes=60 * 1024 * 1024,
        ),
        cost_estimate=pl.CostEstimate(
            flops=10**9, bytes_accessed=3 * 10**6, transcendentals=10**6
        ),
    )(*args)


def solution(mesh):
    rows = P(("dp", "axial"))
    return jax.shard_map(
        local,
        mesh=mesh,
        in_specs=(rows, rows, P("dp"), rows, rows) + (P(),) * 14,
        out_specs=(P("dp", "axial", None), rows),
        check_vma=False,
    )
```

```python
import jax
import jax.numpy as jnp
from jax import lax
from jax.experimental import pallas as pl
from jax.experimental.pallas import tpu as pltpu
from jax.sharding import PartitionSpec as P

N = 16
HEADS = 8
HEAD = 32
INPUTS = 19
F32 = jnp.float32
BF16 = jnp.bfloat16
NN = (((1,), (0,)), ((), ()))
NT = (((1,), (1,)), ((), ()))
TN = (((0,), (0,)), ((), ()))
MESH = pl.DeviceIdType.MESH
NEAR, FAR = (1, 15, 2, 14, 3, 13, 4), (12, 5, 11, 6, 10, 7, 9, 8)
OFFSETS = NEAR + FAR
BIAS, MSA, OPM, TRI, SUM, WIRES = 0, 2, 3, 5, 7, 8


def dot(a, b, dims=NN):
    return lax.dot_general(a, b, dims, preferred_element_type=F32)


def sigmoid(x):
    return 0.5 * jnp.tanh(0.5 * x) + 0.5


def norm(x, axis=-1):
    centred = x - jnp.mean(x, axis=axis, keepdims=True)
    var = jnp.mean(centred * centred, axis=axis, keepdims=True)
    return (centred * lax.rsqrt(var + 1e-05)).astype(BF16)


def iota(shape, axis):
    return lax.broadcasted_iota(jnp.int32, shape, axis)


def ones_where(condition):
    return condition.astype(F32).astype(BF16)


def kernel(*refs):
    n = INPUTS
    body(refs[:n], refs[n], refs[n + 1], refs[n + 2:2 * n + 2], *refs[2 * n + 2:])


def body(
    hbm, msa_out, pair_out, held,
    bias_send, bias_recv, msa_send, msa_recv, opm_send, opm_recv,
    first_send, first_recv, tri_send, tri_recv, sum_send, sum_recv,
    bias_rows, row_x, row_gate, row_v, table_pad, score, head_ones, xr, w2, wt, lift_x, opm_f, tcat,
    right_f, pair_one, tri_n, gate, xt, zt,
    in_sem, send_sem, recv_sem,
):
    (
        act, ids, present, pair, valid, table,
        row_q, row_kvg, bias_w, row_o, col_q, col_kvg, col_o,
        lift, opm_w, tri_w, tri_g, out_g, out_w,
    ) = held
    loads = {
        id(to): pltpu.make_async_copy(at, to, in_sem.at[n])
        for n, (at, to) in enumerate(zip(hbm, held))
    }
    for ref in (pair, bias_w):
        loads[id(ref)].start()

    me = lax.axis_index("axial")
    peers = {r: lax.rem(me + r, N) for r in OFFSETS}
    barrier = pltpu.get_barrier_semaphore()
    for r in OFFSETS:
        pl.semaphore_signal(
            barrier, inc=1, device_id={"axial": peers[r]}, device_id_type=MESH
        )
    for ref in (
        ids, act, table, row_q, row_kvg, present, row_o, opm_w, lift,
        tri_w, tri_g, col_q, col_kvg, col_o, valid, out_g, out_w,
    ):
        loads[id(ref)].start()

    def need(*refs):
        for ref in refs:
            loads.pop(id(ref)).wait()

    wires = {BIAS: (bias_send, bias_recv), BIAS + 1: (bias_send, bias_recv)}
    offsets = {BIAS: NEAR, BIAS + 1: FAR}
    for s in range(1):
        wires[MSA + s] = (msa_send.at[s], msa_recv.at[s])
    for s in range(2):
        wires[OPM + s] = (opm_send.at[s], opm_recv.at[s])
    wires[TRI], wires[TRI + 1] = (first_send, first_recv), (tri_send, tri_recv)
    for s in range(1):
        wires[SUM + s] = (sum_send.at[s], sum_recv.at[s])

    def copy(wire, r, src, dst):
        return pltpu.make_async_remote_copy(
            src_ref=src, dst_ref=dst,
            send_sem=send_sem.at[wire], recv_sem=recv_sem.at[wire],
            device_id={"axial": peers[r]}, device_id_type=MESH,
        )

    def outgoing(wire):
        src, dst = wires[wire]
        whole = BIAS <= wire < MSA or OPM <= wire < TRI
        return [
            copy(wire, r, src if whole else src.at[peers[r]], dst.at[me])
            for r in offsets.get(wire, OFFSETS)
        ]

    def send(wire):
        src, dst = wires[wire]
        for c in outgoing(wire):
            c.start()
        whole = BIAS <= wire < MSA or OPM <= wire < TRI
        if wire != BIAS + 1:
            dst[me] = src[...] if whole else src[me]

    def finish(wire):
        at = wires[wire][1].at[pl.ds(0, len(offsets.get(wire, OFFSETS)))]
        copy(wire, 1, at, at).wait_send()

    def await_all(wire):
        at = wires[wire][1].at[pl.ds(0, len(offsets.get(wire, OFFSETS)))]
        copy(wire, 1, at, at).wait_recv()

    need(pair, bias_w)
    pn = norm(pair[...].astype(F32)).reshape(1024, 128)
    bias_t = dot(bias_w[...], pn, NT)
    for i in range(8):
        bias_rows[pl.ds(i, 8, stride=8), :] = bias_t[:, i * 128:(i + 1) * 128]
    bias_send[...] = bias_rows[...].astype(BF16)
    pl.semaphore_wait(barrier, N - 1)
    send(BIAS)
    send(BIAS + 1)

    need(table, ids, act, row_q, row_kvg)
    head_of = iota((1, 256), 1) // HEAD
    head_mask = [ones_where(head_of == h) for h in range(HEADS)]

    def project(x, wq, wkvg):
        xn = norm(x)
        q = (dot(xn, wq[...]) * HEAD ** -0.5).astype(BF16)
        kvg = dot(xn, wkvg[...])
        return q, kvg[:, :256].astype(BF16), kvg[:, 256:512].astype(BF16), kvg[:, 512:]

    def by_head(a):
        return jnp.concatenate([a * m for m in head_mask], axis=0)

    def mix(scores, extra, v, g):
        parts = []
        for h in range(HEADS):
            one = scores[h * 128:(h + 1) * 128] + extra(h)
            parts.append(jnp.exp(one - jnp.max(one, axis=-1, keepdims=True)).astype(BF16))
        weights = jnp.concatenate(parts, axis=1)
        total = dot(weights, head_ones[...])
        return (dot(weights, by_head(v)) * (sigmoid(g) / total)).astype(BF16)

    table_pad[...] = jnp.zeros((32, 256), F32)
    table_pad[0:23, :] = table[...].astype(F32)
    table_b = table_pad[...].astype(BF16)
    for s in range(2):
        hot = (iota((32, 1), 0) == ids[s:s + 1, :]).astype(F32).T.astype(BF16)
        x = act[s].astype(F32) + dot(hot, table_b)
        q, k, v, g = project(x, row_q, row_kvg)
        score[s] = dot(by_head(q), k, NT)
        row_x[s], row_gate[s], row_v[s] = x, sigmoid(g), by_head(v)

    head_ones[...] = ones_where(iota((1024, 1), 0) // 128 == iota((1, 256), 1) // HEAD)
    need(opm_w, lift, tri_w, tri_g)
    opm_f[...] = opm_w[...].astype(F32)
    for d in range(32):
        w2[:, d * 128:(d + 1) * 128] = opm_f[pl.ds(d, 32, stride=32), :].astype(BF16)
    wt[0:256, :] = tri_w[...].astype(F32).T.astype(BF16)
    wt[256:512, :] = tri_g[...].astype(F32).T.astype(BF16)
    spread = ones_where(iota((64, 1), 0) == 32 + iota((1, 1024), 1) // 32)
    lift_x[...] = dot(lift[...], spread, TN).astype(BF16)

    need(present, row_o, col_q, col_kvg, col_o, valid, out_g, out_w)
    key_bias = 1000000000.0 * (present[...].astype(F32) - 1.0)
    for group in ((0,) + NEAR, FAR):
        await_all(BIAS if group[0] == 0 else BIAS + 1)
        owners = [peers[N - r] if r else me for r in group]
        biases = [bias_recv[p].astype(F32) for p in owners]
        many = len(owners) * 8

        def rows_of(ref, s):
            return jnp.concatenate(
                [ref[s, pl.ds(pl.multiple_of(p * 8, 8), 8), :] for p in owners], axis=0
            )

        weights = []
        for s in range(2):
            parts = []
            for h in range(HEADS):
                one = jnp.concatenate(
                    [
                        score[s, pl.ds(pl.multiple_of(h * 128 + p * 8, 8), 8), :]
                        + (bias[h * 8:(h + 1) * 8] + key_bias)
                        for p, bias in zip(owners, biases)
                    ],
                    axis=0,
                )
                parts.append(jnp.exp(one - jnp.max(one, axis=-1, keepdims=True)).astype(BF16))
            weights.append(jnp.concatenate(parts, axis=1))
        total = dot(jnp.concatenate(weights, axis=0), head_ones[...])
        mixed = jnp.concatenate([dot(weights[s], row_v[s]) for s in range(2)], axis=0)
        gates = jnp.concatenate([rows_of(row_gate, s) for s in range(2)], axis=0)
        heads = (mixed * (gates / total)).astype(BF16)
        x = jnp.concatenate([rows_of(row_x, s) for s in range(2)], axis=0)
        x = x + dot(heads, row_o[...])
        for n, p in enumerate(owners):
            at = (n * 8, n * 8 + many)
            msa_send[0, p] = jnp.concatenate(
                [x[a:a + 8, half * 128:(half + 1) * 128] for a in at for half in range(2)],
                axis=0,
            ).astype(BF16)
        for r, p in zip(group, owners):
            if r:
                copy(MSA, N - r, msa_send.at[0, p], msa_recv.at[0, me]).start()
            else:
                msa_recv[0, me] = msa_send[0, me]

    await_all(MSA)
    for p in range(N):
        block = msa_recv[0, p].astype(F32)
        for s in range(2):
            at = (p * 2 + s) * 8
            for half in range(2):
                xr[half, at:at + 8, :] = block[(s * 2 + half) * 8:(s * 2 + half + 1) * 8]

    own = jnp.where(iota((128, 1), 0) // 32 == iota((1, 128), 1) // 32, 0.0, -jnp.inf)
    own = own.astype(F32)
    keep = iota((128, 1), 0) % 32 == iota((1, 1024), 1) % 32
    done = []
    for n in range(2):
        x = jnp.concatenate(
            [
                jnp.concatenate(
                    [xr[half, pl.ds(n * 4 + l, 32, stride=8), :] for l in range(4)], axis=0
                )
                for half in range(2)
            ],
            axis=1,
        )
        q, k, v, g = project(x, col_q, col_kvg)
        heads = mix(dot(by_head(q), k, NT), lambda h: own, v, g)
        z = (x + dot(heads, col_o[...])).astype(BF16).astype(F32)
        zn = norm(z)
        right = dot(zn, lift_x[...])
        right = jnp.where(keep, right, 0.0).astype(BF16)
        total = jnp.zeros((16, 256), F32)
        for a in range(4):
            pick = ones_where(iota((16, 1), 0) == a * 4 + iota((1, 128), 1) // 32)
            total += dot(pick, right[:, a * 256:(a + 1) * 256])
        opm_send[n] = total.astype(BF16)
        send(OPM + n)
        done.append((z, zn))

    for n in range(2):
        z = done[n][0]
        for half in range(2):
            for l in range(4):
                xr[half, pl.ds(n * 4 + l, 32, stride=8), :] = z[
                    l * 32:(l + 1) * 32, half * 128:(half + 1) * 128
                ]
    for half in range(2):
        msa_out[:, :, half * 128:(half + 1) * 128] = xr[half].reshape(32, 8, 128).astype(BF16)
    zn = jnp.concatenate([done[0][1], done[1][1]], axis=0)
    left = dot(zn, lift[0:32, :], NT).astype(BF16)
    for d in range(0, 32, 2):
        t = dot(left, w2[:, d * 128:(d + 2) * 128]).astype(BF16)
        for i in range(8):
            for e in range(2):
                tcat[(d + e) * 32:(d + e + 1) * 32, i * 128:(i + 1) * 128] = t[
                    i * 32:(i + 1) * 32, e * 128:(e + 1) * 128
                ]

    for n in range(2):
        await_all(OPM + n)
        for p in range(N):
            block = opm_recv[n, p].astype(F32)
            at = p * 8 + n * 4
            for a in range(4):
                right_f[at:at + 4, a * 256:(a + 1) * 256] = block[a * 4:(a + 1) * 4]
    right = right_f[...].astype(BF16)

    for n in range(4):
        update = dot(right, tcat[:, n * 256:(n + 1) * 256])
        for e in range(2):
            i = n * 2 + e
            one = pair[i].astype(F32) + update[:, e * 128:(e + 1) * 128] * (1.0 / 32)
            pair_one[i] = one
            tn = norm(one)
            tri_n[i] = tn
            both = dot(wt[...], tn, NT)
            both = sigmoid(both[256:]) * both[:256] * valid[i:i + 1, :].astype(F32)
            for p in range(N):
                block = jnp.concatenate(
                    [both[p * 8:(p + 1) * 8], both[128 + p * 8:128 + (p + 1) * 8]], axis=0
                )
                if n == 0:
                    first_send[p, :, i * 128:(i + 1) * 128] = block.astype(BF16)
                else:
                    tri_send[p, :, (i - 2) * 128:(i - 1) * 128] = block.astype(BF16)
        if n == 0:
            send(TRI)
    send(TRI + 1)
    for i in range(8):
        gate[i] = sigmoid(dot(tri_n[i], out_g[...]))
    for n, (ref, rows) in enumerate(((first_recv, range(2)), (tri_recv, range(2, 8)))):
        await_all(TRI + n)
        for p in range(N):
            block = ref[p].astype(F32)
            for e, i in enumerate(rows):
                at = (p * 8 + i) * 16
                xt[at:at + 16, :] = block[:, e * 128:(e + 1) * 128]

    for n in range(1):
        sums = []
        for c in range(n * 8, (n + 1) * 8):
            a = xt[pl.ds(c, 128, stride=16), :].astype(BF16)
            b = xt[pl.ds(8 + c, 128, stride=16), :].astype(BF16)
            sums.append(dot(a, b, NT))
        for p in range(N):
            sum_send[n, p] = jnp.concatenate(
                [s[p * 8:(p + 1) * 8] for s in sums], axis=0
            ).astype(BF16)
        send(SUM + n)
    for n in range(1):
        await_all(SUM + n)
        for p in range(N):
            at = (p * 8 + n * 8) * 8
            zt[at:at + 64, :] = sum_recv[n, p].astype(F32)

    for i in range(8):
        mixed = norm(zt[pl.ds(i, 128, stride=8), :], axis=0)
        update = dot(mixed, out_w[...], TN)
        pair_out[i] = (pair_one[i] + gate[i] * update).astype(BF16)
    for wire in wires:
        finish(wire)


def local(*args):
    hbm = pl.BlockSpec(memory_space=pl.ANY)
    vmem = pl.BlockSpec(memory_space=pltpu.VMEM)
    args = list(args)
    args[2] = args[2].reshape(1, 128)
    args[8] = args[8].T
    args[13] = args[13].T
    shapes = (
        pltpu.VMEM((32, 8, 256), BF16),
        pltpu.VMEM((8, 128, 128), BF16),
    )
    return pl.pallas_call(
        kernel,
        out_shape=shapes,
        in_specs=[hbm] * len(args),
        out_specs=(vmem, vmem),
        scratch_shapes=[pltpu.VMEM(a.shape, a.dtype) for a in args] + [
            pltpu.VMEM((64, 128), BF16),
            pltpu.VMEM((N, 64, 128), BF16),
            pltpu.VMEM((1, N, 32, 128), BF16),
            pltpu.VMEM((1, N, 32, 128), BF16),
            pltpu.VMEM((2, 16, 256), BF16),
            pltpu.VMEM((2, N, 16, 256), BF16),
            pltpu.VMEM((N, 16, 256), BF16),
            pltpu.VMEM((N, 16, 256), BF16),
            pltpu.VMEM((N, 16, 768), BF16),
            pltpu.VMEM((N, 16, 768), BF16),
            pltpu.VMEM((1, N, 64, 128), BF16),
            pltpu.VMEM((1, N, 64, 128), BF16),
            pltpu.VMEM((64, 128), F32),
            pltpu.VMEM((2, 128, 256), F32),
            pltpu.VMEM((2, 128, 256), F32),
            pltpu.VMEM((2, 1024, 256), BF16),
            pltpu.VMEM((32, 256), F32),
            pltpu.VMEM((2, 1024, 128), F32),
            pltpu.VMEM((1024, 256), BF16),
            pltpu.VMEM((2, 256, 128), F32),
            pltpu.VMEM((32, 4096), BF16),
            pltpu.VMEM((512, 128), BF16),
            pltpu.VMEM((256, 1024), BF16),
            pltpu.VMEM((1024, 128), F32),
            pltpu.VMEM((1024, 1024), BF16),
            pltpu.VMEM((128, 1024), F32),
            pltpu.VMEM((8, 128, 128), F32),
            pltpu.VMEM((8, 128, 128), BF16),
            pltpu.VMEM((8, 128, 128), F32),
            pltpu.VMEM((2048, 128), F32),
            pltpu.VMEM((1024, 128), F32),
            pltpu.SemaphoreType.DMA((INPUTS,)),
            pltpu.SemaphoreType.DMA((WIRES,)),
            pltpu.SemaphoreType.DMA((WIRES,)),
        ],
        compiler_params=pltpu.CompilerParams(
            collective_id=0, has_side_effects=True, vmem_limit_bytes=60 * 1024 * 1024,
        ),
        cost_estimate=pl.CostEstimate(
            flops=10**9, bytes_accessed=3 * 10**6, transcendentals=10**6
        ),
    )(*args)


def solution(mesh):
    rows = P(("dp", "axial"))
    return jax.shard_map(
        local,
        mesh=mesh,
        in_specs=(rows, rows, P("dp"), rows, rows) + (P(),) * 14,
        out_specs=(P("dp", "axial", None), rows),
        check_vma=False,
    )
```

```python
import jax
import jax.numpy as jnp
from jax import lax
from jax.experimental import pallas as pl
from jax.experimental.pallas import tpu as pltpu
from jax.sharding import PartitionSpec as P

N = 16
HEADS = 8
HEAD = 32
INPUTS = 19
F32 = jnp.float32
BF16 = jnp.bfloat16
NN = (((1,), (0,)), ((), ()))
NT = (((1,), (1,)), ((), ()))
TN = (((0,), (0,)), ((), ()))
MESH = pl.DeviceIdType.MESH
NEAR, FAR = (1, 15, 2, 14, 3, 13, 4), (8, 9, 7, 10, 6, 11, 5, 12)
OFFSETS = NEAR + FAR
BIAS, MSA, OPM, TRI, SUM, WIRES = 0, 2, 3, 5, 7, 8


def dot(a, b, dims=NN):
    return lax.dot_general(a, b, dims, preferred_element_type=F32)


def sigmoid(x):
    return 0.5 * jnp.tanh(0.5 * x) + 0.5


def norm(x, axis=-1):
    centred = x - jnp.mean(x, axis=axis, keepdims=True)
    var = jnp.mean(centred * centred, axis=axis, keepdims=True)
    return (centred * lax.rsqrt(var + 1e-05)).astype(BF16)


def iota(shape, axis):
    return lax.broadcasted_iota(jnp.int32, shape, axis)


def ones_where(condition):
    return condition.astype(F32).astype(BF16)


def kernel(*refs):
    n = INPUTS
    body(refs[:n], refs[n], refs[n + 1], refs[n + 2:2 * n + 2], *refs[2 * n + 2:])


def body(
    hbm, msa_out, pair_out, held,
    bias_send, bias_recv, msa_send, msa_recv, opm_send, opm_recv,
    first_send, first_recv, tri_send, tri_recv, sum_send, sum_recv,
    bias_rows, row_x, row_gate, row_v, table_pad, score, head_ones, xr, w2, wt, lift_x, opm_f, tcat,
    right_f, pair_one, tri_n, gate, xt, zt,
    in_sem, send_sem, recv_sem,
):
    (
        act, ids, present, pair, valid, table,
        row_q, row_kvg, bias_w, row_o, col_q, col_kvg, col_o,
        lift, opm_w, tri_w, tri_g, out_g, out_w,
    ) = held
    loads = {
        id(to): pltpu.make_async_copy(at, to, in_sem.at[n])
        for n, (at, to) in enumerate(zip(hbm, held))
    }
    for ref in (pair, bias_w):
        loads[id(ref)].start()

    me = lax.axis_index("axial")
    peers = {r: lax.rem(me + r, N) for r in OFFSETS}
    barrier = pltpu.get_barrier_semaphore()
    for r in OFFSETS:
        pl.semaphore_signal(
            barrier, inc=1, device_id={"axial": peers[r]}, device_id_type=MESH
        )
    for ref in (
        ids, act, table, row_q, row_kvg, present, row_o, opm_w, lift,
        tri_w, tri_g, col_q, col_kvg, col_o, valid, out_g, out_w,
    ):
        loads[id(ref)].start()

    def need(*refs):
        for ref in refs:
            loads.pop(id(ref)).wait()

    wires = {BIAS: (bias_send, bias_recv), BIAS + 1: (bias_send, bias_recv)}
    far_first = (8, 9, 7, 10, 6, 11, 5, 12, 4, 13, 3, 14, 2, 15, 1)
    offsets = {BIAS: NEAR, BIAS + 1: FAR, OPM: far_first, OPM + 1: far_first, TRI + 1: far_first}
    for s in range(1):
        wires[MSA + s] = (msa_send.at[s], msa_recv.at[s])
    for s in range(2):
        wires[OPM + s] = (opm_send.at[s], opm_recv.at[s])
    wires[TRI], wires[TRI + 1] = (first_send, first_recv), (tri_send, tri_recv)
    for s in range(1):
        wires[SUM + s] = (sum_send.at[s], sum_recv.at[s])

    def copy(wire, r, src, dst):
        return pltpu.make_async_remote_copy(
            src_ref=src, dst_ref=dst,
            send_sem=send_sem.at[wire], recv_sem=recv_sem.at[wire],
            device_id={"axial": peers[r]}, device_id_type=MESH,
        )

    def outgoing(wire):
        src, dst = wires[wire]
        whole = BIAS <= wire < MSA or OPM <= wire < TRI
        return [
            copy(wire, r, src if whole else src.at[peers[r]], dst.at[me])
            for r in offsets.get(wire, OFFSETS)
        ]

    def send(wire):
        src, dst = wires[wire]
        for c in outgoing(wire):
            c.start()
        whole = BIAS <= wire < MSA or OPM <= wire < TRI
        if wire != BIAS + 1:
            dst[me] = src[...] if whole else src[me]

    def finish(wire):
        at = wires[wire][1].at[pl.ds(0, len(offsets.get(wire, OFFSETS)))]
        copy(wire, 1, at, at).wait_send()

    def await_all(wire):
        at = wires[wire][1].at[pl.ds(0, len(offsets.get(wire, OFFSETS)))]
        copy(wire, 1, at, at).wait_recv()

    need(pair, bias_w)
    pn = norm(pair[...].astype(F32)).reshape(1024, 128)
    bias_t = dot(bias_w[...], pn, NT)
    for i in range(8):
        bias_rows[pl.ds(i, 8, stride=8), :] = bias_t[:, i * 128:(i + 1) * 128]
    bias_send[...] = bias_rows[...].astype(BF16)
    pl.semaphore_wait(barrier, N - 1)
    send(BIAS)
    send(BIAS + 1)

    need(table, ids, act, row_q, row_kvg)
    head_of = iota((1, 256), 1) // HEAD
    head_mask = [ones_where(head_of == h) for h in range(HEADS)]

    def project(x, wq, wkvg):
        xn = norm(x)
        q = (dot(xn, wq[...]) * HEAD ** -0.5).astype(BF16)
        kvg = dot(xn, wkvg[...])
        return q, kvg[:, :256].astype(BF16), kvg[:, 256:512].astype(BF16), kvg[:, 512:]

    def by_head(a):
        return jnp.concatenate([a * m for m in head_mask], axis=0)

    def mix(scores, extra, v, g):
        parts = []
        for h in range(HEADS):
            one = scores[h * 128:(h + 1) * 128] + extra(h)
            parts.append(jnp.exp(one - jnp.max(one, axis=-1, keepdims=True)).astype(BF16))
        weights = jnp.concatenate(parts, axis=1)
        total = dot(weights, head_ones[...])
        return (dot(weights, by_head(v)) * (sigmoid(g) / total)).astype(BF16)

    table_pad[...] = jnp.zeros((32, 256), F32)
    table_pad[0:23, :] = table[...].astype(F32)
    table_b = table_pad[...].astype(BF16)
    for s in range(2):
        hot = (iota((32, 1), 0) == ids[s:s + 1, :]).astype(F32).T.astype(BF16)
        x = act[s].astype(F32) + dot(hot, table_b)
        q, k, v, g = project(x, row_q, row_kvg)
        score[s] = dot(by_head(q), k, NT)
        row_x[s], row_gate[s], row_v[s] = x, sigmoid(g), by_head(v)

    head_ones[...] = ones_where(iota((1024, 1), 0) // 128 == iota((1, 256), 1) // HEAD)
    need(opm_w, lift, tri_w, tri_g)
    opm_f[...] = opm_w[...].astype(F32)
    for d in range(32):
        w2[:, d * 128:(d + 1) * 128] = opm_f[pl.ds(d, 32, stride=32), :].astype(BF16)
    wt[0:256, :] = tri_w[...].astype(F32).T.astype(BF16)
    wt[256:512, :] = tri_g[...].astype(F32).T.astype(BF16)
    spread = ones_where(iota((64, 1), 0) == 32 + iota((1, 1024), 1) // 32)
    lift_x[...] = dot(lift[...], spread, TN).astype(BF16)

    need(present, row_o, col_q, col_kvg, col_o, valid, out_g, out_w)
    key_bias = 1000000000.0 * (present[...].astype(F32) - 1.0)
    for group in ((0,) + NEAR, FAR):
        await_all(BIAS if group[0] == 0 else BIAS + 1)
        owners = [peers[N - r] if r else me for r in group]
        biases = [bias_recv[p].astype(F32) for p in owners]
        many = len(owners) * 8

        def rows_of(ref, s):
            return jnp.concatenate(
                [ref[s, pl.ds(pl.multiple_of(p * 8, 8), 8), :] for p in owners], axis=0
            )

        weights = []
        for s in range(2):
            parts = []
            for h in range(HEADS):
                one = jnp.concatenate(
                    [
                        score[s, pl.ds(pl.multiple_of(h * 128 + p * 8, 8), 8), :]
                        + (bias[h * 8:(h + 1) * 8] + key_bias)
                        for p, bias in zip(owners, biases)
                    ],
                    axis=0,
                )
                parts.append(jnp.exp(one - jnp.max(one, axis=-1, keepdims=True)).astype(BF16))
            weights.append(jnp.concatenate(parts, axis=1))
        total = dot(jnp.concatenate(weights, axis=0), head_ones[...])
        mixed = jnp.concatenate([dot(weights[s], row_v[s]) for s in range(2)], axis=0)
        gates = jnp.concatenate([rows_of(row_gate, s) for s in range(2)], axis=0)
        heads = (mixed * (gates / total)).astype(BF16)
        x = jnp.concatenate([rows_of(row_x, s) for s in range(2)], axis=0)
        x = x + dot(heads, row_o[...])
        for n, p in enumerate(owners):
            at = (n * 8, n * 8 + many)
            msa_send[0, p] = jnp.concatenate(
                [x[a:a + 8, half * 128:(half + 1) * 128] for a in at for half in range(2)],
                axis=0,
            ).astype(BF16)
        for r, p in zip(group, owners):
            if r:
                copy(MSA, N - r, msa_send.at[0, p], msa_recv.at[0, me]).start()
            else:
                msa_recv[0, me] = msa_send[0, me]

    await_all(MSA)
    for p in range(N):
        block = msa_recv[0, p].astype(F32)
        for s in range(2):
            at = (p * 2 + s) * 8
            for half in range(2):
                xr[half, at:at + 8, :] = block[(s * 2 + half) * 8:(s * 2 + half + 1) * 8]

    own = jnp.where(iota((128, 1), 0) // 32 == iota((1, 128), 1) // 32, 0.0, -jnp.inf)
    own = own.astype(F32)
    keep = iota((128, 1), 0) % 32 == iota((1, 1024), 1) % 32
    done = []
    for n in range(2):
        x = jnp.concatenate(
            [
                jnp.concatenate(
                    [xr[half, pl.ds(n * 4 + l, 32, stride=8), :] for l in range(4)], axis=0
                )
                for half in range(2)
            ],
            axis=1,
        )
        q, k, v, g = project(x, col_q, col_kvg)
        heads = mix(dot(by_head(q), k, NT), lambda h: own, v, g)
        z = (x + dot(heads, col_o[...])).astype(BF16).astype(F32)
        zn = norm(z)
        right = dot(zn, lift_x[...])
        right = jnp.where(keep, right, 0.0).astype(BF16)
        total = jnp.zeros((16, 256), F32)
        for a in range(4):
            pick = ones_where(iota((16, 1), 0) == a * 4 + iota((1, 128), 1) // 32)
            total += dot(pick, right[:, a * 256:(a + 1) * 256])
        opm_send[n] = total.astype(BF16)
        send(OPM + n)
        done.append((z, zn))

    for n in range(2):
        z = done[n][0]
        for half in range(2):
            for l in range(4):
                xr[half, pl.ds(n * 4 + l, 32, stride=8), :] = z[
                    l * 32:(l + 1) * 32, half * 128:(half + 1) * 128
                ]
    for half in range(2):
        msa_out[:, :, half * 128:(half + 1) * 128] = xr[half].reshape(32, 8, 128).astype(BF16)
    zn = jnp.concatenate([done[0][1], done[1][1]], axis=0)
    left = dot(zn, lift[0:32, :], NT).astype(BF16)
    for d in range(0, 32, 2):
        t = dot(left, w2[:, d * 128:(d + 2) * 128]).astype(BF16)
        for i in range(8):
            for e in range(2):
                tcat[(d + e) * 32:(d + e + 1) * 32, i * 128:(i + 1) * 128] = t[
                    i * 32:(i + 1) * 32, e * 128:(e + 1) * 128
                ]

    for n in range(2):
        await_all(OPM + n)
        for p in range(N):
            block = opm_recv[n, p].astype(F32)
            at = p * 8 + n * 4
            for a in range(4):
                right_f[at:at + 4, a * 256:(a + 1) * 256] = block[a * 4:(a + 1) * 4]
    right = right_f[...].astype(BF16)

    for n in range(4):
        update = dot(right, tcat[:, n * 256:(n + 1) * 256])
        for e in range(2):
            i = n * 2 + e
            one = pair[i].astype(F32) + update[:, e * 128:(e + 1) * 128] * (1.0 / 32)
            pair_one[i] = one
            tn = norm(one)
            tri_n[i] = tn
            both = dot(wt[...], tn, NT)
            both = sigmoid(both[256:]) * both[:256] * valid[i:i + 1, :].astype(F32)
            for p in range(N):
                block = jnp.concatenate(
                    [both[p * 8:(p + 1) * 8], both[128 + p * 8:128 + (p + 1) * 8]], axis=0
                )
                if n == 0:
                    first_send[p, :, i * 128:(i + 1) * 128] = block.astype(BF16)
                else:
                    tri_send[p, :, (i - 2) * 128:(i - 1) * 128] = block.astype(BF16)
        if n == 0:
            send(TRI)
    send(TRI + 1)
    for i in range(8):
        gate[i] = sigmoid(dot(tri_n[i], out_g[...]))
    for n, (ref, rows) in enumerate(((first_recv, range(2)), (tri_recv, range(2, 8)))):
        await_all(TRI + n)
        for p in range(N):
            block = ref[p].astype(F32)
            for e, i in enumerate(rows):
                at = (p * 8 + i) * 16
                xt[at:at + 16, :] = block[:, e * 128:(e + 1) * 128]

    for n in range(1):
        sums = []
        for c in range(n * 8, (n + 1) * 8):
            a = xt[pl.ds(c, 128, stride=16), :].astype(BF16)
            b = xt[pl.ds(8 + c, 128, stride=16), :].astype(BF16)
            sums.append(dot(a, b, NT))
        for p in range(N):
            sum_send[n, p] = jnp.concatenate(
                [s[p * 8:(p + 1) * 8] for s in sums], axis=0
            ).astype(BF16)
        send(SUM + n)
    for n in range(1):
        await_all(SUM + n)
        for p in range(N):
            at = (p * 8 + n * 8) * 8
            zt[at:at + 64, :] = sum_recv[n, p].astype(F32)

    for i in range(8):
        mixed = norm(zt[pl.ds(i, 128, stride=8), :], axis=0)
        update = dot(mixed, out_w[...], TN)
        pair_out[i] = (pair_one[i] + gate[i] * update).astype(BF16)
    for wire in wires:
        finish(wire)


def local(*args):
    hbm = pl.BlockSpec(memory_space=pl.ANY)
    vmem = pl.BlockSpec(memory_space=pltpu.VMEM)
    args = list(args)
    args[2] = args[2].reshape(1, 128)
    args[8] = args[8].T
    args[13] = args[13].T
    shapes = (
        pltpu.VMEM((32, 8, 256), BF16),
        pltpu.VMEM((8, 128, 128), BF16),
    )
    return pl.pallas_call(
        kernel,
        out_shape=shapes,
        in_specs=[hbm] * len(args),
        out_specs=(vmem, vmem),
        scratch_shapes=[pltpu.VMEM(a.shape, a.dtype) for a in args] + [
            pltpu.VMEM((64, 128), BF16),
            pltpu.VMEM((N, 64, 128), BF16),
            pltpu.VMEM((1, N, 32, 128), BF16),
            pltpu.VMEM((1, N, 32, 128), BF16),
            pltpu.VMEM((2, 16, 256), BF16),
            pltpu.VMEM((2, N, 16, 256), BF16),
            pltpu.VMEM((N, 16, 256), BF16),
            pltpu.VMEM((N, 16, 256), BF16),
            pltpu.VMEM((N, 16, 768), BF16),
            pltpu.VMEM((N, 16, 768), BF16),
            pltpu.VMEM((1, N, 64, 128), BF16),
            pltpu.VMEM((1, N, 64, 128), BF16),
            pltpu.VMEM((64, 128), F32),
            pltpu.VMEM((2, 128, 256), F32),
            pltpu.VMEM((2, 128, 256), F32),
            pltpu.VMEM((2, 1024, 256), BF16),
            pltpu.VMEM((32, 256), F32),
            pltpu.VMEM((2, 1024, 128), F32),
            pltpu.VMEM((1024, 256), BF16),
            pltpu.VMEM((2, 256, 128), F32),
            pltpu.VMEM((32, 4096), BF16),
            pltpu.VMEM((512, 128), BF16),
            pltpu.VMEM((256, 1024), BF16),
            pltpu.VMEM((1024, 128), F32),
            pltpu.VMEM((1024, 1024), BF16),
            pltpu.VMEM((128, 1024), F32),
            pltpu.VMEM((8, 128, 128), F32),
            pltpu.VMEM((8, 128, 128), BF16),
            pltpu.VMEM((8, 128, 128), F32),
            pltpu.VMEM((2048, 128), F32),
            pltpu.VMEM((1024, 128), F32),
            pltpu.SemaphoreType.DMA((INPUTS,)),
            pltpu.SemaphoreType.DMA((WIRES,)),
            pltpu.SemaphoreType.DMA((WIRES,)),
        ],
        compiler_params=pltpu.CompilerParams(
            collective_id=0, has_side_effects=True, vmem_limit_bytes=60 * 1024 * 1024,
        ),
        cost_estimate=pl.CostEstimate(
            flops=10**9, bytes_accessed=3 * 10**6, transcendentals=10**6
        ),
    )(*args)


def solution(mesh):
    rows = P(("dp", "axial"))
    return jax.shard_map(
        local,
        mesh=mesh,
        in_specs=(rows, rows, P("dp"), rows, rows) + (P(),) * 14,
        out_specs=(P("dp", "axial", None), rows),
        check_vma=False,
    )
```

```python
import jax
import jax.numpy as jnp
from jax import lax
from jax.experimental import pallas as pl
from jax.experimental.pallas import tpu as pltpu
from jax.sharding import PartitionSpec as P

N = 16
HEADS = 8
HEAD = 32
INPUTS = 19
F32 = jnp.float32
BF16 = jnp.bfloat16
NN = (((1,), (0,)), ((), ()))
NT = (((1,), (1,)), ((), ()))
TN = (((0,), (0,)), ((), ()))
MESH = pl.DeviceIdType.MESH
NEAR, FAR = (1, 15, 2, 14, 3, 13, 4), (8, 9, 7, 10, 6, 11, 5, 12)
OFFSETS = NEAR + FAR
BIAS, MSA, OPM, TRI, SUM, WIRES = 0, 2, 3, 5, 7, 8


def dot(a, b, dims=NN):
    return lax.dot_general(a, b, dims, preferred_element_type=F32)


def sigmoid(x):
    return 0.5 * jnp.tanh(0.5 * x) + 0.5


def norm(x, axis=-1):
    centred = x - jnp.mean(x, axis=axis, keepdims=True)
    var = jnp.mean(centred * centred, axis=axis, keepdims=True)
    return (centred * lax.rsqrt(var + 1e-05)).astype(BF16)


def iota(shape, axis):
    return lax.broadcasted_iota(jnp.int32, shape, axis)


def ones_where(condition):
    return condition.astype(F32).astype(BF16)


def kernel(*refs):
    n = INPUTS
    body(refs[:n], refs[n], refs[n + 1], refs[n + 2:2 * n + 2], *refs[2 * n + 2:])


def body(
    hbm, msa_out, pair_out, held,
    bias_send, bias_recv, msa_send, msa_recv, opm_send, opm_recv,
    first_send, first_recv, tri_send, tri_recv, sum_send, sum_recv,
    bias_rows, row_x, row_gate, row_v, table_pad, score, head_ones, xr, w2, wt, lift_x, opm_f, tcat,
    right_f, pair_one, tri_n, gate, xt, zt,
    in_sem, send_sem, recv_sem,
):
    (
        act, ids, present, pair, valid, table,
        row_q, row_kvg, bias_w, row_o, col_q, col_kvg, col_o,
        lift, opm_w, tri_w, tri_g, out_g, out_w,
    ) = held
    loads = {
        id(to): pltpu.make_async_copy(at, to, in_sem.at[n])
        for n, (at, to) in enumerate(zip(hbm, held))
    }
    for ref in (pair, bias_w):
        loads[id(ref)].start()

    me = lax.axis_index("axial")
    peers = {r: lax.rem(me + r, N) for r in OFFSETS}
    barrier = pltpu.get_barrier_semaphore()
    for r in OFFSETS[::-1]:
        pl.semaphore_signal(
            barrier, inc=1, device_id={"axial": peers[r]}, device_id_type=MESH
        )
    for ref in (
        ids, act, table, row_q, row_kvg, present, row_o, opm_w, lift,
        tri_w, tri_g, col_q, col_kvg, col_o, valid, out_g, out_w,
    ):
        loads[id(ref)].start()

    def need(*refs):
        for ref in refs:
            loads.pop(id(ref)).wait()

    wires = {BIAS: (bias_send, bias_recv), BIAS + 1: (bias_send, bias_recv)}
    far_first = (8, 9, 7, 10, 6, 11, 5, 12, 4, 13, 3, 14, 2, 15, 1)
    offsets = {BIAS: NEAR, BIAS + 1: FAR, OPM: far_first, OPM + 1: far_first, TRI + 1: far_first}
    for s in range(1):
        wires[MSA + s] = (msa_send.at[s], msa_recv.at[s])
    for s in range(2):
        wires[OPM + s] = (opm_send.at[s], opm_recv.at[s])
    wires[TRI], wires[TRI + 1] = (first_send, first_recv), (tri_send, tri_recv)
    for s in range(1):
        wires[SUM + s] = (sum_send.at[s], sum_recv.at[s])

    def copy(wire, r, src, dst):
        return pltpu.make_async_remote_copy(
            src_ref=src, dst_ref=dst,
            send_sem=send_sem.at[wire], recv_sem=recv_sem.at[wire],
            device_id={"axial": peers[r]}, device_id_type=MESH,
        )

    def outgoing(wire):
        src, dst = wires[wire]
        whole = BIAS <= wire < MSA or OPM <= wire < TRI
        return [
            copy(wire, r, src if whole else src.at[peers[r]], dst.at[me])
            for r in offsets.get(wire, OFFSETS)
        ]

    def send(wire):
        src, dst = wires[wire]
        for c in outgoing(wire):
            c.start()
        whole = BIAS <= wire < MSA or OPM <= wire < TRI
        if wire != BIAS + 1:
            dst[me] = src[...] if whole else src[me]

    def finish(wire):
        at = wires[wire][1].at[pl.ds(0, len(offsets.get(wire, OFFSETS)))]
        copy(wire, 1, at, at).wait_send()

    def await_all(wire):
        at = wires[wire][1].at[pl.ds(0, len(offsets.get(wire, OFFSETS)))]
        copy(wire, 1, at, at).wait_recv()

    need(pair, bias_w)
    pn = norm(pair[...].astype(F32)).reshape(1024, 128)
    bias_t = dot(bias_w[...], pn, NT)
    for i in range(8):
        bias_rows[pl.ds(i, 8, stride=8), :] = bias_t[:, i * 128:(i + 1) * 128]
    bias_send[...] = bias_rows[...].astype(BF16)
    pl.semaphore_wait(barrier, N - 1)
    send(BIAS)
    send(BIAS + 1)

    need(table, ids, act, row_q, row_kvg)
    head_of = iota((1, 256), 1) // HEAD
    head_mask = [ones_where(head_of == h) for h in range(HEADS)]

    def project(x, wq, wkvg):
        xn = norm(x)
        q = (dot(xn, wq[...]) * HEAD ** -0.5).astype(BF16)
        kvg = dot(xn, wkvg[...])
        return q, kvg[:, :256].astype(BF16), kvg[:, 256:512].astype(BF16), kvg[:, 512:]

    def by_head(a):
        return jnp.concatenate([a * m for m in head_mask], axis=0)

    def mix(scores, extra, v, g):
        parts = []
        for h in range(HEADS):
            one = scores[h * 128:(h + 1) * 128] + extra(h)
            parts.append(jnp.exp(one - jnp.max(one, axis=-1, keepdims=True)).astype(BF16))
        weights = jnp.concatenate(parts, axis=1)
        total = dot(weights, head_ones[...])
        return (dot(weights, by_head(v)) * (sigmoid(g) / total)).astype(BF16)

    table_pad[...] = jnp.zeros((32, 256), F32)
    table_pad[0:23, :] = table[...].astype(F32)
    table_b = table_pad[...].astype(BF16)
    for s in range(2):
        hot = (iota((32, 1), 0) == ids[s:s + 1, :]).astype(F32).T.astype(BF16)
        x = act[s].astype(F32) + dot(hot, table_b)
        q, k, v, g = project(x, row_q, row_kvg)
        score[s] = dot(by_head(q), k, NT)
        row_x[s], row_gate[s], row_v[s] = x, sigmoid(g), by_head(v)

    head_ones[...] = ones_where(iota((1024, 1), 0) // 128 == iota((1, 256), 1) // HEAD)
    need(opm_w, lift, tri_w, tri_g)
    opm_f[...] = opm_w[...].astype(F32)
    for d in range(32):
        w2[:, d * 128:(d + 1) * 128] = opm_f[pl.ds(d, 32, stride=32), :].astype(BF16)
    wt[0:256, :] = tri_w[...].astype(F32).T.astype(BF16)
    wt[256:512, :] = tri_g[...].astype(F32).T.astype(BF16)
    spread = ones_where(iota((64, 1), 0) == 32 + iota((1, 1024), 1) // 32)
    lift_x[...] = dot(lift[...], spread, TN).astype(BF16)

    need(present, row_o, col_q, col_kvg, col_o, valid, out_g, out_w)
    key_bias = 1000000000.0 * (present[...].astype(F32) - 1.0)
    for group in ((0,) + NEAR, FAR):
        await_all(BIAS if group[0] == 0 else BIAS + 1)
        owners = [peers[N - r] if r else me for r in group]
        biases = [bias_recv[p].astype(F32) for p in owners]
        many = len(owners) * 8

        def rows_of(ref, s):
            return jnp.concatenate(
                [ref[s, pl.ds(pl.multiple_of(p * 8, 8), 8), :] for p in owners], axis=0
            )

        weights = []
        for s in range(2):
            parts = []
            for h in range(HEADS):
                one = jnp.concatenate(
                    [
                        score[s, pl.ds(pl.multiple_of(h * 128 + p * 8, 8), 8), :]
                        + (bias[h * 8:(h + 1) * 8] + key_bias)
                        for p, bias in zip(owners, biases)
                    ],
                    axis=0,
                )
                parts.append(jnp.exp(one - jnp.max(one, axis=-1, keepdims=True)).astype(BF16))
            weights.append(jnp.concatenate(parts, axis=1))
        total = dot(jnp.concatenate(weights, axis=0), head_ones[...])
        mixed = jnp.concatenate([dot(weights[s], row_v[s]) for s in range(2)], axis=0)
        gates = jnp.concatenate([rows_of(row_gate, s) for s in range(2)], axis=0)
        heads = (mixed * (gates / total)).astype(BF16)
        x = jnp.concatenate([rows_of(row_x, s) for s in range(2)], axis=0)
        x = x + dot(heads, row_o[...])
        for n, p in enumerate(owners):
            at = (n * 8, n * 8 + many)
            msa_send[0, p] = jnp.concatenate(
                [x[a:a + 8, half * 128:(half + 1) * 128] for a in at for half in range(2)],
                axis=0,
            ).astype(BF16)
        for r, p in zip(group, owners):
            if r:
                copy(MSA, N - r, msa_send.at[0, p], msa_recv.at[0, me]).start()
            else:
                msa_recv[0, me] = msa_send[0, me]

    await_all(MSA)
    for p in range(N):
        block = msa_recv[0, p].astype(F32)
        for s in range(2):
            at = (p * 2 + s) * 8
            for half in range(2):
                xr[half, at:at + 8, :] = block[(s * 2 + half) * 8:(s * 2 + half + 1) * 8]

    own = jnp.where(iota((128, 1), 0) // 32 == iota((1, 128), 1) // 32, 0.0, -jnp.inf)
    own = own.astype(F32)
    keep = iota((128, 1), 0) % 32 == iota((1, 1024), 1) % 32
    done = []
    for n in range(2):
        x = jnp.concatenate(
            [
                jnp.concatenate(
                    [xr[half, pl.ds(n * 4 + l, 32, stride=8), :] for l in range(4)], axis=0
                )
                for half in range(2)
            ],
            axis=1,
        )
        q, k, v, g = project(x, col_q, col_kvg)
        heads = mix(dot(by_head(q), k, NT), lambda h: own, v, g)
        z = (x + dot(heads, col_o[...])).astype(BF16).astype(F32)
        zn = norm(z)
        right = dot(zn, lift_x[...])
        right = jnp.where(keep, right, 0.0).astype(BF16)
        total = jnp.zeros((16, 256), F32)
        for a in range(4):
            pick = ones_where(iota((16, 1), 0) == a * 4 + iota((1, 128), 1) // 32)
            total += dot(pick, right[:, a * 256:(a + 1) * 256])
        opm_send[n] = total.astype(BF16)
        send(OPM + n)
        done.append((z, zn))

    for n in range(2):
        z = done[n][0]
        for half in range(2):
            for l in range(4):
                xr[half, pl.ds(n * 4 + l, 32, stride=8), :] = z[
                    l * 32:(l + 1) * 32, half * 128:(half + 1) * 128
                ]
    for half in range(2):
        msa_out[:, :, half * 128:(half + 1) * 128] = xr[half].reshape(32, 8, 128).astype(BF16)
    zn = jnp.concatenate([done[0][1], done[1][1]], axis=0)
    left = dot(zn, lift[0:32, :], NT).astype(BF16)
    for d in range(0, 32, 2):
        t = dot(left, w2[:, d * 128:(d + 2) * 128]).astype(BF16)
        for i in range(8):
            for e in range(2):
                tcat[(d + e) * 32:(d + e + 1) * 32, i * 128:(i + 1) * 128] = t[
                    i * 32:(i + 1) * 32, e * 128:(e + 1) * 128
                ]

    for n in range(2):
        await_all(OPM + n)
        for p in range(N):
            block = opm_recv[n, p].astype(F32)
            at = p * 8 + n * 4
            for a in range(4):
                right_f[at:at + 4, a * 256:(a + 1) * 256] = block[a * 4:(a + 1) * 4]
    right = right_f[...].astype(BF16)

    for n in range(4):
        update = dot(right, tcat[:, n * 256:(n + 1) * 256])
        for e in range(2):
            i = n * 2 + e
            one = pair[i].astype(F32) + update[:, e * 128:(e + 1) * 128] * (1.0 / 32)
            pair_one[i] = one
            tn = norm(one)
            tri_n[i] = tn
            both = dot(wt[...], tn, NT)
            both = sigmoid(both[256:]) * both[:256] * valid[i:i + 1, :].astype(F32)
            for p in range(N):
                block = jnp.concatenate(
                    [both[p * 8:(p + 1) * 8], both[128 + p * 8:128 + (p + 1) * 8]], axis=0
                )
                if n == 0:
                    first_send[p, :, i * 128:(i + 1) * 128] = block.astype(BF16)
                else:
                    tri_send[p, :, (i - 2) * 128:(i - 1) * 128] = block.astype(BF16)
        if n == 0:
            send(TRI)
    send(TRI + 1)
    for i in range(8):
        gate[i] = sigmoid(dot(tri_n[i], out_g[...]))
    for n, (ref, rows) in enumerate(((first_recv, range(2)), (tri_recv, range(2, 8)))):
        await_all(TRI + n)
        for p in range(N):
            block = ref[p].astype(F32)
            for e, i in enumerate(rows):
                at = (p * 8 + i) * 16
                xt[at:at + 16, :] = block[:, e * 128:(e + 1) * 128]

    for n in range(1):
        sums = []
        for c in range(n * 8, (n + 1) * 8):
            a = xt[pl.ds(c, 128, stride=16), :].astype(BF16)
            b = xt[pl.ds(8 + c, 128, stride=16), :].astype(BF16)
            sums.append(dot(a, b, NT))
        for p in range(N):
            sum_send[n, p] = jnp.concatenate(
                [s[p * 8:(p + 1) * 8] for s in sums], axis=0
            ).astype(BF16)
        send(SUM + n)
    for n in range(1):
        await_all(SUM + n)
        for p in range(N):
            at = (p * 8 + n * 8) * 8
            zt[at:at + 64, :] = sum_recv[n, p].astype(F32)

    for i in range(8):
        mixed = norm(zt[pl.ds(i, 128, stride=8), :], axis=0)
        update = dot(mixed, out_w[...], TN)
        pair_out[i] = (pair_one[i] + gate[i] * update).astype(BF16)
    for wire in wires:
        finish(wire)


def local(*args):
    hbm = pl.BlockSpec(memory_space=pl.ANY)
    vmem = pl.BlockSpec(memory_space=pltpu.VMEM)
    args = list(args)
    args[2] = args[2].reshape(1, 128)
    args[8] = args[8].T
    args[13] = args[13].T
    shapes = (
        pltpu.VMEM((32, 8, 256), BF16),
        pltpu.VMEM((8, 128, 128), BF16),
    )
    return pl.pallas_call(
        kernel,
        out_shape=shapes,
        in_specs=[hbm] * len(args),
        out_specs=(vmem, vmem),
        scratch_shapes=[pltpu.VMEM(a.shape, a.dtype) for a in args] + [
            pltpu.VMEM((64, 128), BF16),
            pltpu.VMEM((N, 64, 128), BF16),
            pltpu.VMEM((1, N, 32, 128), BF16),
            pltpu.VMEM((1, N, 32, 128), BF16),
            pltpu.VMEM((2, 16, 256), BF16),
            pltpu.VMEM((2, N, 16, 256), BF16),
            pltpu.VMEM((N, 16, 256), BF16),
            pltpu.VMEM((N, 16, 256), BF16),
            pltpu.VMEM((N, 16, 768), BF16),
            pltpu.VMEM((N, 16, 768), BF16),
            pltpu.VMEM((1, N, 64, 128), BF16),
            pltpu.VMEM((1, N, 64, 128), BF16),
            pltpu.VMEM((64, 128), F32),
            pltpu.VMEM((2, 128, 256), F32),
            pltpu.VMEM((2, 128, 256), F32),
            pltpu.VMEM((2, 1024, 256), BF16),
            pltpu.VMEM((32, 256), F32),
            pltpu.VMEM((2, 1024, 128), F32),
            pltpu.VMEM((1024, 256), BF16),
            pltpu.VMEM((2, 256, 128), F32),
            pltpu.VMEM((32, 4096), BF16),
            pltpu.VMEM((512, 128), BF16),
            pltpu.VMEM((256, 1024), BF16),
            pltpu.VMEM((1024, 128), F32),
            pltpu.VMEM((1024, 1024), BF16),
            pltpu.VMEM((128, 1024), F32),
            pltpu.VMEM((8, 128, 128), F32),
            pltpu.VMEM((8, 128, 128), BF16),
            pltpu.VMEM((8, 128, 128), F32),
            pltpu.VMEM((2048, 128), F32),
            pltpu.VMEM((1024, 128), F32),
            pltpu.SemaphoreType.DMA((INPUTS,)),
            pltpu.SemaphoreType.DMA((WIRES,)),
            pltpu.SemaphoreType.DMA((WIRES,)),
        ],
        compiler_params=pltpu.CompilerParams(
            collective_id=0, has_side_effects=True, vmem_limit_bytes=60 * 1024 * 1024,
        ),
        cost_estimate=pl.CostEstimate(
            flops=10**9, bytes_accessed=3 * 10**6, transcendentals=10**6
        ),
    )(*args)


def solution(mesh):
    rows = P(("dp", "axial"))
    return jax.shard_map(
        local,
        mesh=mesh,
        in_specs=(rows, rows, P("dp"), rows, rows) + (P(),) * 14,
        out_specs=(P("dp", "axial", None), rows),
        check_vma=False,
    )
```
